256 devices in a mesh: lev: 16 (over z, y_hi), lon: 16 (over x, y_lo, core).
Axes of the slice: x: 4, y: 4 (y_hi: 2, y_lo: 2; y = y_hi * 2 + y_lo), z: 8, core: 2. Of those that a mesh axis runs over, the one named last changes fastest.
Arguments:
- field: bfloat16 [2, 144, 1536, 256], P(None, 'lev', 'lon'), may hold values from -6 to 6
- eof_basis: bfloat16 [144, 64], replicated, may hold values from -0.5 to 0.5
- band_of_mode: int32 [64], replicated, may hold values from 0 to 7
- coef_table: float32 [8, 256], replicated, may hold values from 0.02 to 0.24
Outputs:
- smoothed: bfloat16 [2, 144, 1536, 256], P(None, 'lev', 'lon')
The draws below stay inside these ranges and needn't reach their ends.
All inputs are finite; a program needn't handle non-finite values.
Results may differ from the reference program's by a relative error of at most 0.013.
Values may be sent and summed in bfloat16 or wider, within the bound.
No kernel may reach another device: no remote copies, remote signals or barrier semaphores. Data moves between devices by JAX's collectives and lax.ppermute only.
A program may use at most 128 MiB of HBM per device.

```python
import math
import jax
import jax.numpy as jnp
from jax import lax

MEM = 2
MODES = 64
LAT = 256
NBAND = 8
STEPS = 8
LEV = 144
NLON = 1536


def place_ends(values, rng, least, top_value):
    longest = values.shape.index(max(values.shape))
    spots = []
    for shift in (0, 1):
        where = [jax.random.randint(jax.random.fold_in(rng, axis), (), 0, length) for axis, length in enumerate(values.shape)]
        where[longest] = (where[longest] + shift) % values.shape[longest]
        spots.append(tuple(where))
    return values.at[spots[0]].set(least).at[spots[1]].set(top_value)


def levels(key, dims, shards, low, largest):
    level, own = 1.0, jax.random.fold_in(key, 6)
    for dim, blocks in shards:
        heights = jnp.exp(jax.random.uniform(jax.random.fold_in(own, dim), (blocks,), jnp.float32, low / len(shards), largest / len(shards)))
        level = level * jnp.repeat(heights, dims[dim] // blocks).reshape([-1 if axis == dim else 1 for axis in range(len(dims))])
    return level


def noise(own_key, extent, spread, bound, split=(), dtype=jnp.bfloat16):
    values = spread * jax.random.normal(own_key, extent, jnp.float32)
    if split:
        values = values * levels(own_key, extent, split, -0.22, 0.18)
    return jnp.clip(values, -bound, bound).astype(dtype)


def setup_inputs(seed: int = 0) -> dict:
    splits = jax.random.split(jax.random.key(seed), 5)
    return {
        "field": noise(splits[0], (MEM, LEV, NLON, LAT), 1.0, 6.0, ((1, 16), (2, 16))),
        "eof_basis": noise(splits[1], (LEV, MODES), LEV ** -0.5, 0.5),
        "band_of_mode": place_ends(jax.random.randint(splits[2], (MODES,), 0, NBAND), jax.random.fold_in(splits[2], 1), 0, NBAND - 1).astype(jnp.int32),
        "coef_table": jnp.clip(jnp.exp(jax.random.uniform(splits[3], (NBAND, LAT), jnp.float32, math.log(0.02), math.log(0.24))), 0.02, 0.24),
    }


def lat_sum(u):
    upper = jnp.pad(u[..., 1:], ((0, 0), (0, 0), (0, 0), (0, 1)))
    lower = jnp.pad(u[..., :-1], ((0, 0), (0, 0), (0, 0), (1, 0)))
    return upper + lower


def reference(field, eof_basis, band_of_mode, coef_table):
    basis = eof_basis.astype(jnp.float32)

    def project(member):
        return jnp.einsum("lk,lxy->kxy", basis, member.astype(jnp.float32)).astype(jnp.bfloat16)

    modes = lax.map(project, field)
    modes = jnp.transpose(modes, (1, 0, 2, 3))
    kappa = coef_table[band_of_mode][:, None, None, :]
    u = modes.astype(jnp.float32)
    for step in range(STEPS):
        neighbours = jnp.roll(u, 1, axis=2) + jnp.roll(u, -1, axis=2) + lat_sum(u)
        u = u + kappa * (neighbours - 4.0 * u)
    diffused = u.astype(jnp.bfloat16).astype(jnp.float32)

    def back(index):
        return jnp.einsum("lk,kxy->lxy", basis, diffused[:, index]).astype(jnp.bfloat16)

    return lax.map(back, jnp.arange(MEM))
```

```python
import jax
import jax.numpy as jnp
from jax import lax
from jax.sharding import PartitionSpec as P

STEPS = 8


def lat_sum(u):
    upper = jnp.pad(u[..., 1:], ((0, 0), (0, 0), (0, 1)))
    lower = jnp.pad(u[..., :-1], ((0, 0), (0, 0), (1, 0)))
    return upper + lower


def loop_pairs(groups, shards, members):
    pieces = groups // members
    pairs = []
    for piece in range(pieces):
        for member in range(members):
            for shard in range(shards):
                here = (piece * members + member) * shards + shard
                if piece + 1 < pieces:
                    there = ((piece + 1) * members + member) * shards + shard
                else:
                    there = member * shards + (shard + 1) % shards
                pairs.append((here, there))
    return pairs


def on_device(field, eof_basis, band_of_mode, coef_table):
    groups, shards = lax.axis_size("lev"), lax.axis_size("lon")
    members, levels, lons, lats = field.shape
    pieces = groups // members
    width = lons // pieces
    cut = field.reshape(members, levels, pieces, width, lats).transpose(2, 0, 1, 3, 4)
    cut = cut.reshape(groups, levels * width, lats)
    whole = lax.all_to_all(cut, "lev", 0, 0, tiled=True).reshape(groups * levels, width, lats)
    modes = jnp.einsum("lk,lxy->xky", eof_basis, whole, preferred_element_type=jnp.float32).astype(jnp.bfloat16)
    onward = loop_pairs(groups, shards, members)
    back = [(b, a) for a, b in onward]
    left = lax.ppermute(modes[width - STEPS :], ("lev", "lon"), onward)
    right = lax.ppermute(modes[:STEPS], ("lev", "lon"), back)
    u = jnp.concatenate([left, modes, right], axis=0).astype(jnp.float32)
    onehot = (band_of_mode[:, None] == jnp.arange(coef_table.shape[0])[None, :]).astype(jnp.float32)
    kappa = jnp.dot(onehot, coef_table, precision=lax.Precision.HIGHEST)
    for step in range(STEPS):
        inner = u[1:-1]
        neighbours = u[2:] + u[:-2] + lat_sum(inner)
        u = inner + kappa * (neighbours - 4.0 * inner)
    diffused = u.astype(jnp.bfloat16)
    total = jnp.einsum("lk,xky->lxy", eof_basis, diffused, preferred_element_type=jnp.float32).astype(jnp.bfloat16)
    total = lax.all_to_all(total.reshape(groups, levels * width, lats), "lev", 0, 0, tiled=True)
    total = total.reshape(pieces, members, levels, width, lats).transpose(1, 2, 0, 3, 4)
    return total.reshape(field.shape)


def solution(mesh):
    return jax.shard_map(
        on_device,
        mesh=mesh,
        in_specs=(P(None, "lev", "lon", None), P(), P(), P()),
        out_specs=P(None, "lev", "lon", None),
        check_vma=False,
    )
```

```python
import functools

import jax
import jax.numpy as jnp
from jax import lax
from jax.experimental import pallas as pl
from jax.experimental.pallas import tpu as pltpu
from jax.sharding import PartitionSpec as P

STEPS = 8
ROWS = 16
SPLITS = 1
LANES = 128


def place(piece, shard, pieces):
    return piece + (shard % 2) * (pieces - 1 - 2 * piece)


def loop_pairs(groups, shards, members):
    pieces = groups // members
    pairs = []
    for shard in range(shards):
        for piece in range(pieces):
            for member in range(members):
                carry, after = divmod(piece + 1, pieces)
                then = (shard + carry) % shards
                here = place(piece, shard, pieces) * members + member
                there = place(after, then, pieces) * members + member
                pairs.append((here * shards + shard, there * shards + then))
    return pairs


def pack_kernel(pieces, field_ref, out_ref, held_ref, sems):
    members, levels, lons, lats = field_ref.shape
    width = lons // pieces
    shard = lax.axis_index("lon")
    copies = []
    for level in range(levels):
        for member in range(members):
            copy = pltpu.make_async_copy(field_ref.at[member, level], held_ref.at[member, level], sems.at[member, level])
            copy.start()
            copies.append(copy)
    for level in range(levels):
        for member in range(members):
            copies[level * members + member].wait()
            for piece in range(pieces):
                to = place(piece, shard, pieces) * members + member
                out_ref[to, level * width : (level + 1) * width, :] = held_ref[
                    member, level, piece * width : (piece + 1) * width, :
                ]


def pack(field, pieces):
    members, levels, lons, lats = field.shape
    return pl.pallas_call(
        functools.partial(pack_kernel, pieces),
        out_shape=jax.ShapeDtypeStruct((pieces * members, levels * (lons // pieces), lats), field.dtype),
        in_specs=[pl.BlockSpec(memory_space=pl.ANY)],
        out_specs=pl.BlockSpec(memory_space=pltpu.VMEM),
        scratch_shapes=[pltpu.VMEM(field.shape, field.dtype), pltpu.SemaphoreType.DMA((members, levels))],
        compiler_params=pltpu.CompilerParams(vmem_limit_bytes=16 * 1024 * 1024),
        name="pack",
    )(field)


def unpack_kernel(pieces, blocks_ref, out_ref, held_ref, sems):
    members, levels, lons, lats = out_ref.shape
    width = lons // pieces
    shard = lax.axis_index("lon")
    copies = []
    for level in range(levels):
        for member in range(members):
            for piece in range(pieces):
                at = place(piece, shard, pieces) * members + member
                held_ref[member, level, piece * width : (piece + 1) * width, :] = blocks_ref[
                    at, level * width : (level + 1) * width, :
                ]
            copy = pltpu.make_async_copy(held_ref.at[member, level], out_ref.at[member, level], sems.at[member, level])
            copy.start()
            copies.append(copy)
    for copy in copies:
        copy.wait()


def unpack(blocks, shape, pieces):
    members, levels, lons, lats = shape
    return pl.pallas_call(
        functools.partial(unpack_kernel, pieces),
        out_shape=jax.ShapeDtypeStruct(shape, blocks.dtype),
        in_specs=[pl.BlockSpec(memory_space=pltpu.VMEM)],
        out_specs=pl.BlockSpec(memory_space=pl.ANY),
        scratch_shapes=[pltpu.VMEM(shape, blocks.dtype), pltpu.SemaphoreType.DMA((members, levels))],
        compiler_params=pltpu.CompilerParams(vmem_limit_bytes=16 * 1024 * 1024),
        name="unpack",
    )(blocks)


def lat_sum(halves, first, last):
    ups = [pltpu.roll(half, 1, 1) for half in halves]
    downs = [pltpu.roll(half, LANES - 1, 1) for half in halves]
    out = []
    for i in range(len(halves)):
        below = ups[i - 1] if i else 0.0
        above = downs[i + 1] if i + 1 < len(halves) else 0.0
        out.append(jnp.where(first, below, ups[i]) + jnp.where(last, above, downs[i]))
    return out


def diffuse(modes_ref, left_ref, right_ref, kappa_ref, out_ref, u_ref):
    width, count, lats = modes_ref.shape
    tiles = lats // LANES
    lane = lax.broadcasted_iota(jnp.int32, (ROWS, LANES), 1)
    first, last = lane == 0, lane == LANES - 1

    def cut(x):
        return [x[:, i * LANES : (i + 1) * LANES] for i in range(tiles)]

    def block(index, carry):
        rows = pl.ds(pl.multiple_of(index * ROWS, ROWS), ROWS)
        kappa = cut(kappa_ref[rows, :])
        keep = [1.0 - 4.0 * k for k in kappa]
        total = width + 2 * STEPS

        def start(column):
            if column < STEPS:
                ref, at = left_ref, column
            elif column < STEPS + width:
                ref, at = modes_ref, column - STEPS
            else:
                ref, at = right_ref, column - STEPS - width
            return cut(ref[at, rows, :].astype(jnp.float32))

        for step in range(STEPS):
            get = start if step == 0 else (lambda column: cut(u_ref[column]))
            before, here = get(step), get(step + 1)
            for column in range(step + 1, total - step - 1):
                after = get(column + 1)
                sides = lat_sum(here, first, last)
                new = [
                    c * h + k * ((b + a) + s)
                    for c, h, k, b, a, s in zip(keep, here, kappa, before, after, sides)
                ]
                new = jnp.concatenate(new, axis=1)
                if step + 1 < STEPS:
                    u_ref[column] = new
                else:
                    out_ref[column - STEPS, rows, :] = new.astype(out_ref.dtype)
                before, here = here, after
        return carry

    lax.fori_loop(0, count // ROWS, block, 0)


def diffused(modes, left, right, kappa):
    width, count, lats = modes.shape
    return pl.pallas_call(
        diffuse,
        out_shape=jax.ShapeDtypeStruct(modes.shape, jnp.bfloat16),
        in_specs=[pl.BlockSpec(memory_space=pltpu.VMEM)] * 4,
        out_specs=pl.BlockSpec(memory_space=pltpu.VMEM),
        scratch_shapes=[pltpu.VMEM((width + 2 * STEPS, ROWS, lats), jnp.float32)],
        compiler_params=pltpu.CompilerParams(vmem_limit_bytes=16 * 1024 * 1024),
        cost_estimate=pl.CostEstimate(flops=60 * count * lats * (width + STEPS), bytes_accessed=6 * count * lats * width, transcendentals=0),
        name="diffuse",
    )(modes, left, right, kappa)


def on_device(field, eof_basis, band_of_mode, coef_table):
    groups, shards = lax.axis_size("lev"), lax.axis_size("lon")
    members, levels, lons, lats = field.shape
    pieces = groups // members
    width = lons // pieces
    count = eof_basis.shape[1]
    cut = pack(field, pieces)
    whole = lax.all_to_all(cut, "lev", 0, 0, tiled=True).reshape(groups * levels, width, lats)
    modes = jnp.einsum("lk,lxy->xky", eof_basis, whole, preferred_element_type=jnp.float32).astype(jnp.bfloat16)
    onward = loop_pairs(groups, shards, members)
    back = [(b, a) for a, b in onward]
    onehot = (band_of_mode[:, None] == jnp.arange(coef_table.shape[0])[None, :]).astype(jnp.float32)
    kappa = jnp.dot(onehot, coef_table, precision=lax.Precision.HIGHEST)
    share = count // SPLITS
    parts = []
    for split in range(SPLITS):
        some = modes[:, split * share : (split + 1) * share]
        left = lax.ppermute(some[width - STEPS :], ("lev", "lon"), onward)
        right = lax.ppermute(some[:STEPS], ("lev", "lon"), back)
        parts.append(diffused(some, left, right, kappa[split * share : (split + 1) * share]))
    final = jnp.concatenate(parts, axis=1) if SPLITS > 1 else parts[0]
    total = jnp.einsum("lk,xky->lxy", eof_basis, final, preferred_element_type=jnp.float32).astype(jnp.bfloat16)
    total = lax.all_to_all(total.reshape(groups, levels * width, lats), "lev", 0, 0, tiled=True)
    return unpack(total, field.shape, pieces)


def solution(mesh):
    return jax.shard_map(
        on_device,
        mesh=mesh,
        in_specs=(P(None, "lev", "lon", None), P(), P(), P()),
        out_specs=P(None, "lev", "lon", None),
        check_vma=False,
    )
```

```python
import functools

import jax
import jax.numpy as jnp
from jax import lax
from jax.experimental import pallas as pl
from jax.experimental.pallas import tpu as pltpu
from jax.sharding import PartitionSpec as P

STEPS = 8
ROWS = 16
SPLITS = 2
LANES = 128


def place(piece, shard, pieces):
    return piece + (shard % 2) * (pieces - 1 - 2 * piece)


def loop_pairs(groups, shards, members):
    pieces = groups // members
    pairs = []
    for shard in range(shards):
        for piece in range(pieces):
            for member in range(members):
                carry, after = divmod(piece + 1, pieces)
                then = (shard + carry) % shards
                here = place(piece, shard, pieces) * members + member
                there = place(after, then, pieces) * members + member
                pairs.append((here * shards + shard, there * shards + then))
    return pairs


def sending_order(pieces):
    return list(range(0, pieces, 2)) + list(range(1, pieces, 2))


def slot(member, piece, pieces):
    return member * pieces + sending_order(pieces).index(piece)


def owners(shard, pieces, members):
    return [place(piece, shard, pieces) * members + member for member in range(members) for piece in sending_order(pieces)]


def exchange(blocks, groups, shards, members):
    order = [[lev * shards + shard for lev in owners(shard, groups // members, members)] for shard in range(shards)]
    return lax.all_to_all(blocks, ("lev", "lon"), 0, 0, tiled=True, axis_index_groups=order)


def basis_by_owner(basis, groups, members):
    rows = basis.shape[0] // groups

    def ordered(shard):
        return jnp.concatenate([basis[lev * rows : (lev + 1) * rows] for lev in owners(shard, groups // members, members)])

    return jnp.where(lax.axis_index("lon") % 2 == 0, ordered(0), ordered(1))


def pack_kernel(pieces, field_ref, out_ref):
    members, levels, lons, lats = field_ref.shape
    width = lons // pieces
    for level in range(levels):
        for member in range(members):
            for piece in range(pieces):
                out_ref[slot(member, piece, pieces), level * width : (level + 1) * width, :] = field_ref[
                    member, level, piece * width : (piece + 1) * width, :
                ]


def pack(field, pieces):
    members, levels, lons, lats = field.shape
    return pl.pallas_call(
        functools.partial(pack_kernel, pieces),
        out_shape=jax.ShapeDtypeStruct((pieces * members, levels * (lons // pieces), lats), field.dtype),
        in_specs=[pl.BlockSpec(memory_space=pltpu.VMEM)],
        out_specs=pl.BlockSpec(memory_space=pltpu.VMEM),
        compiler_params=pltpu.CompilerParams(vmem_limit_bytes=16 * 1024 * 1024),
        name="pack",
    )(field)


def unpack_kernel(pieces, blocks_ref, out_ref, held_ref, sems):
    members, levels, lons, lats = out_ref.shape
    width = lons // pieces
    copies = []
    for level in range(levels):
        for member in range(members):
            for piece in range(pieces):
                held_ref[member, level, piece * width : (piece + 1) * width, :] = blocks_ref[
                    slot(member, piece, pieces), level * width : (level + 1) * width, :
                ]
            copy = pltpu.make_async_copy(held_ref.at[member, level], out_ref.at[member, level], sems.at[member, level])
            copy.start()
            copies.append(copy)
    for copy in copies:
        copy.wait()


def unpack(blocks, shape, pieces):
    members, levels, lons, lats = shape
    return pl.pallas_call(
        functools.partial(unpack_kernel, pieces),
        out_shape=jax.ShapeDtypeStruct(shape, blocks.dtype),
        in_specs=[pl.BlockSpec(memory_space=pltpu.VMEM)],
        out_specs=pl.BlockSpec(memory_space=pl.ANY),
        scratch_shapes=[pltpu.VMEM(shape, blocks.dtype), pltpu.SemaphoreType.DMA((members, levels))],
        compiler_params=pltpu.CompilerParams(vmem_limit_bytes=16 * 1024 * 1024),
        name="unpack",
    )(blocks)


def lat_sum(halves, first, last):
    ups = [pltpu.roll(half, 1, 1) for half in halves]
    downs = [pltpu.roll(half, LANES - 1, 1) for half in halves]
    out = []
    for i in range(len(halves)):
        below = ups[i - 1] if i else 0.0
        above = downs[i + 1] if i + 1 < len(halves) else 0.0
        out.append(jnp.where(first, below, ups[i]) + jnp.where(last, above, downs[i]))
    return out


def diffuse(modes_ref, left_ref, right_ref, kappa_ref, out_ref, u_ref):
    width, count, lats = modes_ref.shape
    tiles = lats // LANES
    lane = lax.broadcasted_iota(jnp.int32, (ROWS, LANES), 1)
    first, last = lane == 0, lane == LANES - 1

    def cut(x):
        return [x[:, i * LANES : (i + 1) * LANES] for i in range(tiles)]

    def block(index, carry):
        rows = pl.ds(pl.multiple_of(index * ROWS, ROWS), ROWS)
        kappa = cut(kappa_ref[rows, :])
        keep = [1.0 - 4.0 * k for k in kappa]
        total = width + 2 * STEPS

        def start(column):
            if column < STEPS:
                ref, at = left_ref, column
            elif column < STEPS + width:
                ref, at = modes_ref, column - STEPS
            else:
                ref, at = right_ref, column - STEPS - width
            return cut(ref[at, rows, :].astype(jnp.float32))

        for step in range(STEPS):
            get = start if step == 0 else (lambda column: cut(u_ref[column]))
            before, here = get(step), get(step + 1)
            for column in range(step + 1, total - step - 1):
                after = get(column + 1)
                sides = lat_sum(here, first, last)
                new = [
                    c * h + k * ((b + a) + s)
                    for c, h, k, b, a, s in zip(keep, here, kappa, before, after, sides)
                ]
                new = jnp.concatenate(new, axis=1)
                if step + 1 < STEPS:
                    u_ref[column] = new
                else:
                    out_ref[column - STEPS, rows, :] = new.astype(out_ref.dtype)
                before, here = here, after
        return carry

    lax.fori_loop(0, count // ROWS, block, 0)


def diffused(modes, left, right, kappa):
    width, count, lats = modes.shape
    return pl.pallas_call(
        diffuse,
        out_shape=jax.ShapeDtypeStruct(modes.shape, jnp.bfloat16),
        in_specs=[pl.BlockSpec(memory_space=pltpu.VMEM)] * 4,
        out_specs=pl.BlockSpec(memory_space=pltpu.VMEM),
        scratch_shapes=[pltpu.VMEM((width + 2 * STEPS, ROWS, lats), jnp.float32)],
        compiler_params=pltpu.CompilerParams(vmem_limit_bytes=16 * 1024 * 1024),
        cost_estimate=pl.CostEstimate(flops=60 * count * lats * (width + STEPS), bytes_accessed=6 * count * lats * width, transcendentals=0),
        name="diffuse",
    )(modes, left, right, kappa)


def on_device(field, eof_basis, band_of_mode, coef_table):
    groups, shards = lax.axis_size("lev"), lax.axis_size("lon")
    members, levels, lons, lats = field.shape
    pieces = groups // members
    width = lons // pieces
    count = eof_basis.shape[1]
    basis = basis_by_owner(eof_basis, groups, members)
    cut = pack(field, pieces)
    whole = exchange(cut, groups, shards, members).reshape(groups * levels, width, lats)
    modes = jnp.einsum("lk,lxy->xky", basis, whole, preferred_element_type=jnp.float32).astype(jnp.bfloat16)
    onward = loop_pairs(groups, shards, members)
    back = [(b, a) for a, b in onward]
    onehot = (band_of_mode[:, None] == jnp.arange(coef_table.shape[0])[None, :]).astype(jnp.float32)
    kappa = jnp.dot(onehot, coef_table, precision=lax.Precision.HIGHEST)
    share = count // SPLITS
    parts = []
    for split in range(SPLITS):
        some = modes[:, split * share : (split + 1) * share]
        left = lax.ppermute(some[width - STEPS :], ("lev", "lon"), onward)
        right = lax.ppermute(some[:STEPS], ("lev", "lon"), back)
        parts.append(diffused(some, left, right, kappa[split * share : (split + 1) * share]))
    final = jnp.concatenate(parts, axis=1) if SPLITS > 1 else parts[0]
    total = jnp.einsum("lk,xky->lxy", basis, final, preferred_element_type=jnp.float32).astype(jnp.bfloat16)
    total = exchange(total.reshape(groups, levels * width, lats), groups, shards, members)
    return unpack(total, field.shape, pieces)


def solution(mesh):
    return jax.shard_map(
        on_device,
        mesh=mesh,
        in_specs=(P(None, "lev", "lon", None), P(), P(), P()),
        out_specs=P(None, "lev", "lon", None),
        check_vma=False,
    )
```

```python
import functools

import jax
import jax.numpy as jnp
from jax import lax
from jax.experimental import pallas as pl
from jax.experimental.pallas import tpu as pltpu
from jax.sharding import PartitionSpec as P

STEPS = 8
LANES = 128
THERE = (1, 4, 6, 12, 2, 8, 11, 14, 0, 10, 9, 13, 3, 7, 5, 15)
BACK = (1, 7, 6, 12, 2, 8, 11, 14, 0, 10, 9, 13, 3, 4, 5, 15)
SPLITS = 2


def place(piece, shard, pieces):
    return piece + (shard % 2) * (pieces - 1 - 2 * piece)


def loop_pairs(groups, shards, members):
    pieces = groups // members
    pairs = []
    for shard in range(shards):
        for piece in range(pieces):
            for member in range(members):
                carry, after = divmod(piece + 1, pieces)
                then = (shard + carry) % shards
                here = place(piece, shard, pieces) * members + member
                there = place(after, then, pieces) * members + member
                pairs.append((here * shards + shard, there * shards + then))
    return pairs


def slot(order, member, piece, members):
    return order.index(piece * members + member)


def owners(order, shard, pieces, members):
    return [place(cell // members, shard, pieces) * members + cell % members for cell in order]


def exchange(order, blocks, groups, shards, members):
    devices = [[lev * shards + shard for lev in owners(order, shard, groups // members, members)] for shard in range(shards)]
    return lax.all_to_all(blocks, ("lev", "lon"), 0, 0, tiled=True, axis_index_groups=devices)


def basis_by_owner(order, basis, groups, members):
    rows = basis.shape[0] // groups

    def ordered(shard):
        found = owners(order, shard, groups // members, members)
        return jnp.concatenate([basis[lev * rows : (lev + 1) * rows] for lev in found])

    return jnp.where(lax.axis_index("lon") % 2 == 0, ordered(0), ordered(1))


def pack_kernel(pieces, field_ref, out_ref):
    members, levels, lons, lats = field_ref.shape
    width = lons // pieces
    for level in range(levels):
        for member in range(members):
            for piece in range(pieces):
                out_ref[slot(THERE, member, piece, members), level * width : (level + 1) * width, :] = field_ref[
                    member, level, piece * width : (piece + 1) * width, :
                ]


def pack(field, pieces):
    members, levels, lons, lats = field.shape
    return pl.pallas_call(
        functools.partial(pack_kernel, pieces),
        out_shape=jax.ShapeDtypeStruct((pieces * members, levels * (lons // pieces), lats), field.dtype),
        in_specs=[pl.BlockSpec(memory_space=pltpu.VMEM)],
        out_specs=pl.BlockSpec(memory_space=pltpu.VMEM),
        compiler_params=pltpu.CompilerParams(vmem_limit_bytes=16 * 1024 * 1024),
        name="pack",
    )(field)


def unpack_kernel(pieces, blocks_ref, out_ref, held_ref, sems):
    members, levels, lons, lats = out_ref.shape
    width = lons // pieces
    copies = []
    for level in range(levels):
        for member in range(members):
            for piece in range(pieces):
                at = slot(BACK, member, piece, members)
                for half in range(lats // LANES):
                    row = (half * levels + level) * width
                    columns = slice(half * LANES, (half + 1) * LANES)
                    held_ref[member, level, piece * width : (piece + 1) * width, columns] = blocks_ref[at, row : row + width, :]
            copy = pltpu.make_async_copy(held_ref.at[member, level], out_ref.at[member, level], sems.at[member, level])
            copy.start()
            copies.append(copy)
    for copy in copies:
        copy.wait()


def unpack(blocks, shape, pieces):
    members, levels, lons, lats = shape
    return pl.pallas_call(
        functools.partial(unpack_kernel, pieces),
        out_shape=jax.ShapeDtypeStruct(shape, blocks.dtype),
        in_specs=[pl.BlockSpec(memory_space=pltpu.VMEM)],
        out_specs=pl.BlockSpec(memory_space=pl.ANY),
        scratch_shapes=[pltpu.VMEM(shape, blocks.dtype), pltpu.SemaphoreType.DMA((members, levels))],
        compiler_params=pltpu.CompilerParams(vmem_limit_bytes=16 * 1024 * 1024),
        name="unpack",
    )(blocks)


def paired(lats):
    row = lax.broadcasted_iota(jnp.int32, (lats, lats), 0)
    column = lax.broadcasted_iota(jnp.int32, (lats, lats), 1)
    half = lats // 2
    to = jnp.where(column < half, 2 * column, 2 * (column - half) + 1)
    back = jnp.where(row < half, 2 * row, 2 * (row - half) + 1)
    spread = jnp.where(row == to, 1.0, 0.0).astype(jnp.bfloat16)
    gather = jnp.where(column == back, 1.0, 0.0).astype(jnp.bfloat16)
    return spread, gather


def diffuse(modes_ref, left_ref, right_ref, kappa_ref, out_ref, u_ref, v_ref):
    width, count, lats = modes_ref.shape
    half = lats // 2
    total = width + 2 * STEPS
    spread, gather = paired(lats)

    def load(ref, at):
        cells = ref[...].reshape(ref.shape[0] * count, lats)
        cells = jnp.dot(cells, spread, preferred_element_type=jnp.float32)
        u_ref[at : at + ref.shape[0]] = cells.reshape(ref.shape[0], count, lats)

    load(left_ref, 0)
    load(modes_ref, STEPS)
    load(right_ref, STEPS + width)
    lane = lax.broadcasted_iota(jnp.int32, (count, half), 1)
    first, last = lane == 0, lane == half - 1
    kappa = kappa_ref[:, :half], kappa_ref[:, half:]
    keep = 1.0 - 4.0 * kappa[0], 1.0 - 4.0 * kappa[1]
    old, new = u_ref, v_ref
    for step in range(STEPS):
        before = old[step, :, :half], old[step, :, half:]
        here = old[step + 1, :, :half], old[step + 1, :, half:]
        for column in range(step + 1, total - step - 1):
            after = old[column + 1, :, :half], old[column + 1, :, half:]
            even, odd = here
            beside_even = odd + jnp.where(first, 0.0, pltpu.roll(odd, 1, 1))
            beside_odd = even + jnp.where(last, 0.0, pltpu.roll(even, half - 1, 1))
            new[column, :, :half] = keep[0] * even + kappa[0] * ((before[0] + after[0]) + beside_even)
            new[column, :, half:] = keep[1] * odd + kappa[1] * ((before[1] + after[1]) + beside_odd)
            before, here = here, after
        old, new = new, old
    cells = old[STEPS : STEPS + width].astype(jnp.bfloat16).reshape(width * count, lats)
    cells = jnp.dot(cells, gather, preferred_element_type=jnp.float32)
    out_ref[...] = cells.astype(out_ref.dtype).reshape(width, count, lats)


def diffused(modes, left, right, kappa):
    width, count, lats = modes.shape
    cells = pltpu.VMEM((width + 2 * STEPS, count, lats), jnp.float32)
    return pl.pallas_call(
        diffuse,
        out_shape=jax.ShapeDtypeStruct(modes.shape, jnp.bfloat16),
        in_specs=[pl.BlockSpec(memory_space=pltpu.VMEM)] * 4,
        out_specs=pl.BlockSpec(memory_space=pltpu.VMEM),
        scratch_shapes=[cells, cells],
        compiler_params=pltpu.CompilerParams(vmem_limit_bytes=16 * 1024 * 1024),
        cost_estimate=pl.CostEstimate(flops=60 * count * lats * (width + STEPS), bytes_accessed=6 * count * lats * width, transcendentals=0),
        name="diffuse",
    )(modes, left, right, kappa)


def on_device(field, eof_basis, band_of_mode, coef_table):
    groups, shards = lax.axis_size("lev"), lax.axis_size("lon")
    members, levels, lons, lats = field.shape
    pieces = groups // members
    width = lons // pieces
    count = eof_basis.shape[1]
    basis = basis_by_owner(THERE, eof_basis, groups, members)
    basis_back = basis_by_owner(BACK, eof_basis, groups, members)
    cut = pack(field, pieces)
    whole = exchange(THERE, cut, groups, shards, members).reshape(groups * levels, width, lats)
    modes = jnp.einsum("lk,lxy->xky", basis, whole, preferred_element_type=jnp.float32).astype(jnp.bfloat16)
    onward = loop_pairs(groups, shards, members)
    back = [(b, a) for a, b in onward]
    onehot = (band_of_mode[:, None] == jnp.arange(coef_table.shape[0])[None, :]).astype(jnp.float32)
    pairs = coef_table.reshape(-1, lats // 2, 2).transpose(0, 2, 1).reshape(coef_table.shape)
    kappa = jnp.dot(onehot, pairs, precision=lax.Precision.HIGHEST)
    share = count // SPLITS
    parts = []
    for split in range(SPLITS):
        some = modes[:, split * share : (split + 1) * share]
        left = lax.ppermute(some[width - STEPS :], ("lev", "lon"), onward)
        right = lax.ppermute(some[:STEPS], ("lev", "lon"), back)
        parts.append(diffused(some, left, right, kappa[split * share : (split + 1) * share]))
    final = jnp.concatenate(parts, axis=1) if SPLITS > 1 else parts[0]
    total = jnp.einsum("lk,xky->lxy", basis_back, final, preferred_element_type=jnp.float32).astype(jnp.bfloat16)
    total = total.reshape(groups, levels * width, lats // LANES, LANES).transpose(0, 2, 1, 3).reshape(groups, -1, LANES)
    total = exchange(BACK, total, groups, shards, members)
    return unpack(total, field.shape, pieces)


def solution(mesh):
    return jax.shard_map(
        on_device,
        mesh=mesh,
        in_specs=(P(None, "lev", "lon", None), P(), P(), P()),
        out_specs=P(None, "lev", "lon", None),
        check_vma=False,
    )
```

```python
import functools

import jax
import jax.numpy as jnp
from jax import lax
from jax.experimental import pallas as pl
from jax.experimental.pallas import tpu as pltpu
from jax.sharding import PartitionSpec as P

STEPS = 8
LANES = 128
THERE = (1, 4, 6, 12, 2, 8, 11, 14, 0, 10, 9, 13, 3, 7, 5, 15)
BACK = (1, 7, 6, 12, 2, 8, 11, 14, 0, 10, 9, 13, 3, 4, 5, 15)
SPLITS = 2


def place(piece, shard, pieces):
    return piece + (shard % 2) * (pieces - 1 - 2 * piece)


def loop_pairs(groups, shards, members):
    pieces = groups // members
    pairs = []
    for shard in range(shards):
        for piece in range(pieces):
            for member in range(members):
                carry, after = divmod(piece + 1, pieces)
                then = (shard + carry) % shards
                here = place(piece, shard, pieces) * members + member
                there = place(after, then, pieces) * members + member
                pairs.append((here * shards + shard, there * shards + then))
    return pairs


def slot(order, member, piece, members):
    return order.index(piece * members + member)


def owners(order, shard, pieces, members):
    return [place(cell // members, shard, pieces) * members + cell % members for cell in order]


def exchange(order, blocks, groups, shards, members):
    devices = [[lev * shards + shard for lev in owners(order, shard, groups // members, members)] for shard in range(shards)]
    return lax.all_to_all(blocks, ("lev", "lon"), 0, 0, tiled=True, axis_index_groups=devices)


def basis_by_owner(order, basis, groups, members):
    rows = basis.shape[0] // groups

    def ordered(shard):
        found = owners(order, shard, groups // members, members)
        return jnp.concatenate([basis[lev * rows : (lev + 1) * rows] for lev in found])

    return jnp.where(lax.axis_index("lon") % 2 == 0, ordered(0), ordered(1))


def pack_kernel(pieces, field_ref, out_ref):
    members, levels, lons, lats = field_ref.shape
    width = lons // pieces
    for level in range(levels):
        for member in range(members):
            for piece in range(pieces):
                to = slot(THERE, member, piece, members)
                for half in range(lats // LANES):
                    row = (half * levels + level) * width
                    columns = slice(half * LANES, (half + 1) * LANES)
                    out_ref[to, row : row + width, :] = field_ref[member, level, piece * width : (piece + 1) * width, columns]


def pack(field, pieces):
    members, levels, lons, lats = field.shape
    return pl.pallas_call(
        functools.partial(pack_kernel, pieces),
        out_shape=jax.ShapeDtypeStruct((pieces * members, levels * (lons // pieces) * lats // LANES, LANES), field.dtype),
        in_specs=[pl.BlockSpec(memory_space=pltpu.VMEM)],
        out_specs=pl.BlockSpec(memory_space=pltpu.VMEM),
        compiler_params=pltpu.CompilerParams(vmem_limit_bytes=16 * 1024 * 1024),
        name="pack",
    )(field)


def unpack_kernel(pieces, blocks_ref, out_ref, held_ref, sems):
    members, levels, lons, lats = out_ref.shape
    width = lons // pieces
    copies = []
    for level in range(levels):
        for member in range(members):
            for piece in range(pieces):
                at = slot(BACK, member, piece, members)
                for half in range(lats // LANES):
                    row = (half * levels + level) * width
                    columns = slice(half * LANES, (half + 1) * LANES)
                    held_ref[member, level, piece * width : (piece + 1) * width, columns] = blocks_ref[at, row : row + width, :]
            copy = pltpu.make_async_copy(held_ref.at[member, level], out_ref.at[member, level], sems.at[member, level])
            copy.start()
            copies.append(copy)
    for copy in copies:
        copy.wait()


def unpack(blocks, shape, pieces):
    members, levels, lons, lats = shape
    return pl.pallas_call(
        functools.partial(unpack_kernel, pieces),
        out_shape=jax.ShapeDtypeStruct(shape, blocks.dtype),
        in_specs=[pl.BlockSpec(memory_space=pltpu.VMEM)],
        out_specs=pl.BlockSpec(memory_space=pl.ANY),
        scratch_shapes=[pltpu.VMEM(shape, blocks.dtype), pltpu.SemaphoreType.DMA((members, levels))],
        compiler_params=pltpu.CompilerParams(vmem_limit_bytes=16 * 1024 * 1024),
        name="unpack",
    )(blocks)


def doubled(basis, groups):
    rows = basis.reshape(groups, 1, -1, 1, basis.shape[1])
    same = jnp.eye(2, dtype=basis.dtype).reshape(1, 2, 1, 2, 1)
    return (rows * same).reshape(2 * basis.shape[0], 2 * basis.shape[1])


def project_kernel(width, blocks_ref, basis_ref, *refs):
    outs, held_ref = refs[:-1], refs[-1]
    groups, rows, lanes = blocks_ref.shape
    modes = basis_ref.shape[0] // 2
    share = modes // SPLITS
    for block in range(groups):
        held_ref[block * rows : (block + 1) * rows, :] = blocks_ref[block].astype(jnp.float32)
    for column in range(width):
        levels = held_ref[pl.ds(column, groups * rows // width, stride=width), :].astype(jnp.bfloat16)
        cells = jnp.dot(basis_ref[...], levels, preferred_element_type=jnp.float32).astype(jnp.bfloat16)
        cells = jnp.concatenate([cells[:modes], cells[modes:]], axis=1)
        for split in range(SPLITS):
            part = cells[split * share : (split + 1) * share]
            whole_ref, tail_ref, head_ref = outs[3 * split : 3 * split + 3]
            whole_ref[column] = part
            if column >= width - STEPS:
                tail_ref[column - width + STEPS] = part
            if column < STEPS:
                head_ref[column] = part


def project(blocks, basis, width):
    groups, rows, lanes = blocks.shape
    share = basis.shape[0] // 2 // SPLITS
    shapes = [jax.ShapeDtypeStruct((columns, share, 2 * lanes), jnp.bfloat16) for columns in (width, STEPS, STEPS)]
    return pl.pallas_call(
        functools.partial(project_kernel, width),
        out_shape=shapes * SPLITS,
        in_specs=[pl.BlockSpec(memory_space=pltpu.VMEM)] * 2,
        out_specs=[pl.BlockSpec(memory_space=pltpu.VMEM)] * (3 * SPLITS),
        scratch_shapes=[pltpu.VMEM((groups * rows, lanes), jnp.float32)],
        compiler_params=pltpu.CompilerParams(vmem_limit_bytes=16 * 1024 * 1024),
        name="project",
    )(blocks, basis)


def expand_kernel(groups, basis_ref, *refs):
    parts, out_ref, held_ref = refs[:SPLITS], refs[SPLITS], refs[SPLITS + 1]
    width = parts[0].shape[0]
    rows, lanes = out_ref.shape[1:]
    for column in range(width):
        cells = [part[column, :, half * lanes : (half + 1) * lanes] for half in range(2) for part in parts]
        cells = jnp.concatenate(cells, axis=0)
        levels = jnp.dot(basis_ref[...], cells, preferred_element_type=jnp.float32)
        held_ref[pl.ds(column, groups * rows // width, stride=width), :] = levels
    for block in range(groups):
        out_ref[block] = held_ref[block * rows : (block + 1) * rows, :].astype(out_ref.dtype)


def expand(parts, basis, groups):
    width, share, lats = parts[0].shape
    rows = basis.shape[0] * width // groups
    return pl.pallas_call(
        functools.partial(expand_kernel, groups),
        out_shape=jax.ShapeDtypeStruct((groups, rows, lats // 2), jnp.bfloat16),
        in_specs=[pl.BlockSpec(memory_space=pltpu.VMEM)] * (SPLITS + 1),
        out_specs=pl.BlockSpec(memory_space=pltpu.VMEM),
        scratch_shapes=[pltpu.VMEM((groups * rows, lats // 2), jnp.float32)],
        compiler_params=pltpu.CompilerParams(vmem_limit_bytes=16 * 1024 * 1024),
        name="expand",
    )(basis, *parts)


def paired(lats):
    row = lax.broadcasted_iota(jnp.int32, (lats, lats), 0)
    column = lax.broadcasted_iota(jnp.int32, (lats, lats), 1)
    half = lats // 2
    to = jnp.where(column < half, 2 * column, 2 * (column - half) + 1)
    back = jnp.where(row < half, 2 * row, 2 * (row - half) + 1)
    spread = jnp.where(row == to, 1.0, 0.0).astype(jnp.bfloat16)
    gather = jnp.where(column == back, 1.0, 0.0).astype(jnp.bfloat16)
    return spread, gather


def diffuse(modes_ref, left_ref, right_ref, kappa_ref, out_ref, u_ref, v_ref):
    width, count, lats = modes_ref.shape
    half = lats // 2
    total = width + 2 * STEPS
    spread, gather = paired(lats)

    def load(ref, at):
        cells = ref[...].reshape(ref.shape[0] * count, lats)
        cells = jnp.dot(cells, spread, preferred_element_type=jnp.float32)
        u_ref[at : at + ref.shape[0]] = cells.reshape(ref.shape[0], count, lats)

    load(left_ref, 0)
    load(modes_ref, STEPS)
    load(right_ref, STEPS + width)
    lane = lax.broadcasted_iota(jnp.int32, (count, half), 1)
    first, last = lane == 0, lane == half - 1
    kappa = kappa_ref[:, :half], kappa_ref[:, half:]
    keep = 1.0 - 4.0 * kappa[0], 1.0 - 4.0 * kappa[1]
    old, new = u_ref, v_ref
    for step in range(STEPS):
        before = old[step, :, :half], old[step, :, half:]
        here = old[step + 1, :, :half], old[step + 1, :, half:]
        for column in range(step + 1, total - step - 1):
            after = old[column + 1, :, :half], old[column + 1, :, half:]
            even, odd = here
            beside_even = odd + jnp.where(first, 0.0, pltpu.roll(odd, 1, 1))
            beside_odd = even + jnp.where(last, 0.0, pltpu.roll(even, half - 1, 1))
            new[column, :, :half] = keep[0] * even + kappa[0] * ((before[0] + after[0]) + beside_even)
            new[column, :, half:] = keep[1] * odd + kappa[1] * ((before[1] + after[1]) + beside_odd)
            before, here = here, after
        old, new = new, old
    cells = old[STEPS : STEPS + width].astype(jnp.bfloat16).reshape(width * count, lats)
    cells = jnp.dot(cells, gather, preferred_element_type=jnp.float32)
    out_ref[...] = cells.astype(out_ref.dtype).reshape(width, count, lats)


def diffused(modes, left, right, kappa):
    width, count, lats = modes.shape
    cells = pltpu.VMEM((width + 2 * STEPS, count, lats), jnp.float32)
    return pl.pallas_call(
        diffuse,
        out_shape=jax.ShapeDtypeStruct(modes.shape, jnp.bfloat16),
        in_specs=[pl.BlockSpec(memory_space=pltpu.VMEM)] * 4,
        out_specs=pl.BlockSpec(memory_space=pltpu.VMEM),
        scratch_shapes=[cells, cells],
        compiler_params=pltpu.CompilerParams(vmem_limit_bytes=16 * 1024 * 1024),
        cost_estimate=pl.CostEstimate(flops=60 * count * lats * (width + STEPS), bytes_accessed=6 * count * lats * width, transcendentals=0),
        name="diffuse",
    )(modes, left, right, kappa)


def on_device(field, eof_basis, band_of_mode, coef_table):
    groups, shards = lax.axis_size("lev"), lax.axis_size("lon")
    members, levels, lons, lats = field.shape
    pieces = groups // members
    width = lons // pieces
    count = eof_basis.shape[1]
    basis = basis_by_owner(THERE, eof_basis, groups, members)
    basis_back = basis_by_owner(BACK, eof_basis, groups, members)
    cut = pack(field, pieces)
    whole = exchange(THERE, cut, groups, shards, members)
    modes = project(whole, doubled(basis, groups).T, width)
    onward = loop_pairs(groups, shards, members)
    back = [(b, a) for a, b in onward]
    onehot = (band_of_mode[:, None] == jnp.arange(coef_table.shape[0])[None, :]).astype(jnp.float32)
    pairs = coef_table.reshape(-1, lats // 2, 2).transpose(0, 2, 1).reshape(coef_table.shape)
    kappa = jnp.dot(onehot, pairs, precision=lax.Precision.HIGHEST)
    share = count // SPLITS
    parts = []
    for split in range(SPLITS):
        some, tail, head = modes[3 * split : 3 * split + 3]
        left = lax.ppermute(tail, ("lev", "lon"), onward)
        right = lax.ppermute(head, ("lev", "lon"), back)
        parts.append(diffused(some, left, right, kappa[split * share : (split + 1) * share]))
    total = expand(parts, doubled(basis_back, groups), groups)
    total = exchange(BACK, total, groups, shards, members)
    return unpack(total, field.shape, pieces)


def solution(mesh):
    return jax.shard_map(
        on_device,
        mesh=mesh,
        in_specs=(P(None, "lev", "lon", None), P(), P(), P()),
        out_specs=P(None, "lev", "lon", None),
        check_vma=False,
    )
```

```python
import functools

import jax
import jax.numpy as jnp
from jax import lax
from jax.experimental import pallas as pl
from jax.experimental.pallas import tpu as pltpu
from jax.sharding import PartitionSpec as P

STEPS = 8
LANES = 128
THERE = (15, 10, 8, 2, 12, 6, 5, 0, 14, 4, 9, 11, 13, 7, 3, 1)
BACK = (15, 10, 8, 2, 12, 6, 5, 0, 14, 4, 7, 3, 13, 9, 11, 1)
SPLITS = 2


def place(piece, shard, pieces):
    return piece + ((shard + 1) % 2) * (pieces - 1 - 2 * piece)


def loop_pairs(groups, shards, members):
    pieces = groups // members
    pairs = []
    for shard in range(shards):
        for piece in range(pieces):
            for member in range(members):
                carry, after = divmod(piece + 1, pieces)
                then = (shard + carry) % shards
                here = place(piece, shard, pieces) * members + member
                there = place(after, then, pieces) * members + member
                pairs.append((here * shards + shard, there * shards + then))
    return pairs


def slot(order, member, piece, members):
    return order.index(piece * members + member)


def owners(order, shard, pieces, members):
    return [place(cell // members, shard, pieces) * members + cell % members for cell in order]


def exchange(order, blocks, groups, shards, members):
    devices = [[lev * shards + shard for lev in owners(order, shard, groups // members, members)] for shard in range(shards)]
    return lax.all_to_all(blocks, ("lev", "lon"), 0, 0, tiled=True, axis_index_groups=devices)


def basis_by_owner(order, basis, groups, members):
    rows = basis.shape[0] // groups

    def ordered(shard):
        found = owners(order, shard, groups // members, members)
        return jnp.concatenate([basis[lev * rows : (lev + 1) * rows] for lev in found])

    return jnp.where(lax.axis_index("lon") % 2 == 0, ordered(0), ordered(1))


def pack_kernel(pieces, field_ref, out_ref, held_ref, sems):
    members, levels, lons, lats = field_ref.shape
    width = lons // pieces
    copies = []
    for member in range(members):
        for piece in range(pieces):
            to = slot(THERE, member, piece, members)
            for level in range(levels):
                for half in range(lats // LANES):
                    row = (half * levels + level) * width
                    columns = slice(half * LANES, (half + 1) * LANES)
                    held_ref[to, row : row + width, :] = field_ref[member, level, piece * width : (piece + 1) * width, columns]
            copy = pltpu.make_async_copy(held_ref.at[to], out_ref.at[to], sems.at[to])
            copy.start()
            copies.append(copy)
    for copy in copies:
        copy.wait()


def pack(field, pieces):
    members, levels, lons, lats = field.shape
    shape = (pieces * members, levels * (lons // pieces) * lats // LANES, LANES)
    return pl.pallas_call(
        functools.partial(pack_kernel, pieces),
        out_shape=jax.ShapeDtypeStruct(shape, field.dtype),
        in_specs=[pl.BlockSpec(memory_space=pltpu.VMEM)],
        out_specs=pl.BlockSpec(memory_space=pl.ANY),
        scratch_shapes=[pltpu.VMEM(shape, field.dtype), pltpu.SemaphoreType.DMA((pieces * members,))],
        compiler_params=pltpu.CompilerParams(vmem_limit_bytes=16 * 1024 * 1024),
        name="pack",
    )(field)


def unpack_kernel(pieces, blocks_ref, out_ref, held_ref, sems):
    members, levels, lons, lats = out_ref.shape
    width = lons // pieces
    copies = []
    for level in range(levels):
        for member in range(members):
            for piece in range(pieces):
                at = slot(BACK, member, piece, members)
                for half in range(lats // LANES):
                    row = (half * levels + level) * width
                    columns = slice(half * LANES, (half + 1) * LANES)
                    held_ref[member, level, piece * width : (piece + 1) * width, columns] = blocks_ref[at, row : row + width, :]
            copy = pltpu.make_async_copy(held_ref.at[member, level], out_ref.at[member, level], sems.at[member, level])
            copy.start()
            copies.append(copy)
    for copy in copies:
        copy.wait()


def unpack(blocks, shape, pieces):
    members, levels, lons, lats = shape
    return pl.pallas_call(
        functools.partial(unpack_kernel, pieces),
        out_shape=jax.ShapeDtypeStruct(shape, blocks.dtype),
        in_specs=[pl.BlockSpec(memory_space=pltpu.VMEM)],
        out_specs=pl.BlockSpec(memory_space=pl.ANY),
        scratch_shapes=[pltpu.VMEM(shape, blocks.dtype), pltpu.SemaphoreType.DMA((members, levels))],
        compiler_params=pltpu.CompilerParams(vmem_limit_bytes=16 * 1024 * 1024),
        name="unpack",
    )(blocks)


def doubled(basis, groups):
    rows = basis.reshape(groups, 1, -1, 1, basis.shape[1])
    same = jnp.eye(2, dtype=basis.dtype).reshape(1, 2, 1, 2, 1)
    return (rows * same).reshape(2 * basis.shape[0], 2 * basis.shape[1])


def project_kernel(width, blocks_ref, basis_ref, *refs):
    outs, held_ref = refs[:-1], refs[-1]
    groups, rows, lanes = blocks_ref.shape
    modes = basis_ref.shape[0] // 2
    share = modes // SPLITS
    for block in range(groups):
        held_ref[block * rows : (block + 1) * rows, :] = blocks_ref[block].astype(jnp.float32)
    for column in range(width):
        levels = held_ref[pl.ds(column, groups * rows // width, stride=width), :].astype(jnp.bfloat16)
        cells = jnp.dot(basis_ref[...], levels, preferred_element_type=jnp.float32).astype(jnp.bfloat16)
        cells = jnp.concatenate([cells[:modes], cells[modes:]], axis=1)
        for split in range(SPLITS):
            part = cells[split * share : (split + 1) * share]
            whole_ref, tail_ref, head_ref = outs[3 * split : 3 * split + 3]
            whole_ref[column] = part
            if column >= width - STEPS:
                tail_ref[column - width + STEPS] = part
            if column < STEPS:
                head_ref[column] = part


def project(blocks, basis, width):
    groups, rows, lanes = blocks.shape
    share = basis.shape[0] // 2 // SPLITS
    shapes = [jax.ShapeDtypeStruct((columns, share, 2 * lanes), jnp.bfloat16) for columns in (width, STEPS, STEPS)]
    return pl.pallas_call(
        functools.partial(project_kernel, width),
        out_shape=shapes * SPLITS,
        in_specs=[pl.BlockSpec(memory_space=pltpu.VMEM)] * 2,
        out_specs=[pl.BlockSpec(memory_space=pltpu.VMEM)] * (3 * SPLITS),
        scratch_shapes=[pltpu.VMEM((groups * rows, lanes), jnp.float32)],
        compiler_params=pltpu.CompilerParams(vmem_limit_bytes=16 * 1024 * 1024),
        name="project",
    )(blocks, basis)


def expand_kernel(groups, basis_ref, *refs):
    parts, out_ref, held_ref = refs[:SPLITS], refs[SPLITS], refs[SPLITS + 1]
    width = parts[0].shape[0]
    rows, lanes = out_ref.shape[1:]
    for column in range(width):
        cells = [part[column, :, half * lanes : (half + 1) * lanes] for half in range(2) for part in parts]
        cells = jnp.concatenate(cells, axis=0)
        levels = jnp.dot(basis_ref[...], cells, preferred_element_type=jnp.float32)
        held_ref[pl.ds(column, groups * rows // width, stride=width), :] = levels
    for block in range(groups):
        out_ref[block] = held_ref[block * rows : (block + 1) * rows, :].astype(out_ref.dtype)


def expand(parts, basis, groups):
    width, share, lats = parts[0].shape
    rows = basis.shape[0] * width // groups
    return pl.pallas_call(
        functools.partial(expand_kernel, groups),
        out_shape=jax.ShapeDtypeStruct((groups, rows, lats // 2), jnp.bfloat16),
        in_specs=[pl.BlockSpec(memory_space=pltpu.VMEM)] * (SPLITS + 1),
        out_specs=pl.BlockSpec(memory_space=pltpu.VMEM),
        scratch_shapes=[pltpu.VMEM((groups * rows, lats // 2), jnp.float32)],
        compiler_params=pltpu.CompilerParams(vmem_limit_bytes=16 * 1024 * 1024),
        name="expand",
    )(basis, *parts)


def paired(lats):
    row = lax.broadcasted_iota(jnp.int32, (lats, lats), 0)
    column = lax.broadcasted_iota(jnp.int32, (lats, lats), 1)
    half = lats // 2
    to = jnp.where(column < half, 2 * column, 2 * (column - half) + 1)
    back = jnp.where(row < half, 2 * row, 2 * (row - half) + 1)
    spread = jnp.where(row == to, 1.0, 0.0).astype(jnp.bfloat16)
    gather = jnp.where(column == back, 1.0, 0.0).astype(jnp.bfloat16)
    return spread, gather


def diffuse(modes_ref, left_ref, right_ref, kappa_ref, out_ref, u_ref, v_ref):
    width, count, lats = modes_ref.shape
    half = lats // 2
    total = width + 2 * STEPS
    spread, gather = paired(lats)

    def load(ref, at):
        cells = ref[...].reshape(ref.shape[0] * count, lats)
        cells = jnp.dot(cells, spread, preferred_element_type=jnp.float32)
        u_ref[at : at + ref.shape[0]] = cells.reshape(ref.shape[0], count, lats)

    load(left_ref, 0)
    load(modes_ref, STEPS)
    load(right_ref, STEPS + width)
    lane = lax.broadcasted_iota(jnp.int32, (count, half), 1)
    first, last = lane == 0, lane == half - 1
    kappa = kappa_ref[:, :half], kappa_ref[:, half:]
    keep = 1.0 - 4.0 * kappa[0], 1.0 - 4.0 * kappa[1]
    old, new = u_ref, v_ref
    for step in range(STEPS):
        before = old[step, :, :half], old[step, :, half:]
        here = old[step + 1, :, :half], old[step + 1, :, half:]
        for column in range(step + 1, total - step - 1):
            after = old[column + 1, :, :half], old[column + 1, :, half:]
            even, odd = here
            beside_even = odd + jnp.where(first, 0.0, pltpu.roll(odd, 1, 1))
            beside_odd = even + jnp.where(last, 0.0, pltpu.roll(even, half - 1, 1))
            new[column, :, :half] = keep[0] * even + kappa[0] * ((before[0] + after[0]) + beside_even)
            new[column, :, half:] = keep[1] * odd + kappa[1] * ((before[1] + after[1]) + beside_odd)
            before, here = here, after
        old, new = new, old
    cells = old[STEPS : STEPS + width].astype(jnp.bfloat16).reshape(width * count, lats)
    cells = jnp.dot(cells, gather, preferred_element_type=jnp.float32)
    out_ref[...] = cells.astype(out_ref.dtype).reshape(width, count, lats)


def diffused(modes, left, right, kappa):
    width, count, lats = modes.shape
    cells = pltpu.VMEM((width + 2 * STEPS, count, lats), jnp.float32)
    return pl.pallas_call(
        diffuse,
        out_shape=jax.ShapeDtypeStruct(modes.shape, jnp.bfloat16),
        in_specs=[pl.BlockSpec(memory_space=pltpu.VMEM)] * 4,
        out_specs=pl.BlockSpec(memory_space=pltpu.VMEM),
        scratch_shapes=[cells, cells],
        compiler_params=pltpu.CompilerParams(vmem_limit_bytes=16 * 1024 * 1024),
        cost_estimate=pl.CostEstimate(flops=60 * count * lats * (width + STEPS), bytes_accessed=6 * count * lats * width, transcendentals=0),
        name="diffuse",
    )(modes, left, right, kappa)


def on_device(field, eof_basis, band_of_mode, coef_table):
    groups, shards = lax.axis_size("lev"), lax.axis_size("lon")
    members, levels, lons, lats = field.shape
    pieces = groups // members
    width = lons // pieces
    count = eof_basis.shape[1]
    basis = basis_by_owner(THERE, eof_basis, groups, members)
    basis_back = basis_by_owner(BACK, eof_basis, groups, members)
    cut = pack(field, pieces)
    whole = exchange(THERE, cut, groups, shards, members)
    modes = project(whole, doubled(basis, groups).T, width)
    onward = loop_pairs(groups, shards, members)
    back = [(b, a) for a, b in onward]
    onehot = (band_of_mode[:, None] == jnp.arange(coef_table.shape[0])[None, :]).astype(jnp.float32)
    pairs = coef_table.reshape(-1, lats // 2, 2).transpose(0, 2, 1).reshape(coef_table.shape)
    kappa = jnp.dot(onehot, pairs, precision=lax.Precision.HIGHEST)
    share = count // SPLITS
    parts = []
    for split in range(SPLITS):
        some, tail, head = modes[3 * split : 3 * split + 3]
        left = lax.ppermute(tail, ("lev", "lon"), onward)
        right = lax.ppermute(head, ("lev", "lon"), back)
        parts.append(diffused(some, left, right, kappa[split * share : (split + 1) * share]))
    total = expand(parts, doubled(basis_back, groups), groups)
    total = exchange(BACK, total, groups, shards, members)
    return unpack(total, field.shape, pieces)


def solution(mesh):
    return jax.shard_map(
        on_device,
        mesh=mesh,
        in_specs=(P(None, "lev", "lon", None), P(), P(), P()),
        out_specs=P(None, "lev", "lon", None),
        check_vma=False,
    )
```

```python
import functools

import jax
import jax.numpy as jnp
from jax import lax
from jax.experimental import pallas as pl
from jax.experimental.pallas import tpu as pltpu
from jax.sharding import PartitionSpec as P

STEPS = 8
LANES = 128
SPARE = 16
THERE = (15, 10, 8, 2, 12, 6, 5, 0, 14, 4, 9, 11, 13, 7, 3, 1)
BACK = (15, 10, 8, 2, 12, 6, 5, 0, 14, 4, 7, 3, 13, 9, 11, 1)
SPLITS = 2


def place(piece, shard, pieces):
    return piece + ((shard + 1) % 2) * (pieces - 1 - 2 * piece)


def loop_pairs(groups, shards, members):
    pieces = groups // members
    pairs = []
    for shard in range(shards):
        for piece in range(pieces):
            for member in range(members):
                carry, after = divmod(piece + 1, pieces)
                then = (shard + carry) % shards
                here = place(piece, shard, pieces) * members + member
                there = place(after, then, pieces) * members + member
                pairs.append((here * shards + shard, there * shards + then))
    return pairs


def slot(order, member, piece, members):
    return order.index(piece * members + member)


def owners(order, shard, pieces, members):
    return [place(cell // members, shard, pieces) * members + cell % members for cell in order]


def exchange(order, blocks, groups, shards, members):
    devices = [[lev * shards + shard for lev in owners(order, shard, groups // members, members)] for shard in range(shards)]
    return lax.all_to_all(blocks, ("lev", "lon"), 0, 0, tiled=True, axis_index_groups=devices)


def basis_by_owner(order, basis, groups, members):
    rows = basis.shape[0] // groups

    def ordered(shard):
        found = owners(order, shard, groups // members, members)
        return jnp.concatenate([basis[lev * rows : (lev + 1) * rows] for lev in found])

    return jnp.where(lax.axis_index("lon") % 2 == 0, ordered(0), ordered(1))


def pack_kernel(pieces, field_ref, out_ref, held_ref, sems):
    members, levels, lons, lats = field_ref.shape
    width = lons // pieces
    copies = []
    for member in range(members):
        for piece in range(pieces):
            to = slot(THERE, member, piece, members)
            for level in range(levels):
                for half in range(lats // LANES):
                    row = (half * levels + level) * width
                    columns = slice(half * LANES, (half + 1) * LANES)
                    held_ref[to, row : row + width, :] = field_ref[member, level, piece * width : (piece + 1) * width, columns]
            copy = pltpu.make_async_copy(held_ref.at[to], out_ref.at[to], sems.at[to])
            copy.start()
            copies.append(copy)
    for copy in copies:
        copy.wait()


def pack(field, pieces):
    members, levels, lons, lats = field.shape
    shape = (pieces * members, levels * (lons // pieces) * lats // LANES, LANES)
    return pl.pallas_call(
        functools.partial(pack_kernel, pieces),
        out_shape=jax.ShapeDtypeStruct(shape, field.dtype),
        in_specs=[pl.BlockSpec(memory_space=pltpu.VMEM)],
        out_specs=pl.BlockSpec(memory_space=pl.ANY),
        scratch_shapes=[pltpu.VMEM(shape, field.dtype), pltpu.SemaphoreType.DMA((pieces * members,))],
        compiler_params=pltpu.CompilerParams(vmem_limit_bytes=16 * 1024 * 1024),
        name="pack",
    )(field)


def unpack_kernel(pieces, blocks_ref, out_ref, held_ref, sems):
    members, levels, lons, lats = out_ref.shape
    width = lons // pieces
    copies = []
    for level in range(levels):
        for member in range(members):
            for piece in range(pieces):
                at = slot(BACK, member, piece, members)
                for half in range(lats // LANES):
                    row = (half * levels + level) * width
                    columns = slice(half * LANES, (half + 1) * LANES)
                    held_ref[member, level, piece * width : (piece + 1) * width, columns] = blocks_ref[at, row : row + width, :]
            copy = pltpu.make_async_copy(held_ref.at[member, level], out_ref.at[member, level], sems.at[member, level])
            copy.start()
            copies.append(copy)
    for copy in copies:
        copy.wait()


def unpack(blocks, shape, pieces):
    members, levels, lons, lats = shape
    return pl.pallas_call(
        functools.partial(unpack_kernel, pieces),
        out_shape=jax.ShapeDtypeStruct(shape, blocks.dtype),
        in_specs=[pl.BlockSpec(memory_space=pltpu.VMEM)],
        out_specs=pl.BlockSpec(memory_space=pl.ANY),
        scratch_shapes=[pltpu.VMEM(shape, blocks.dtype), pltpu.SemaphoreType.DMA((members, levels))],
        compiler_params=pltpu.CompilerParams(vmem_limit_bytes=16 * 1024 * 1024),
        name="unpack",
    )(blocks)


def doubled(basis, groups):
    rows = basis.reshape(groups, 1, -1, 1, basis.shape[1])
    same = jnp.eye(2, dtype=basis.dtype).reshape(1, 2, 1, 2, 1)
    return (rows * same).reshape(2 * basis.shape[0], 2 * basis.shape[1])


def project_kernel(width, blocks_ref, basis_ref, *refs):
    outs, held_ref = refs[:-1], refs[-1]
    groups, rows, lanes = blocks_ref.shape
    modes = basis_ref.shape[0] // 2
    share = modes // SPLITS
    for block in range(groups):
        held_ref[block * rows : (block + 1) * rows, :] = blocks_ref[block].astype(jnp.float32)
    for column in range(width):
        levels = held_ref[pl.ds(column, groups * rows // width, stride=width), :].astype(jnp.bfloat16)
        cells = jnp.dot(basis_ref[...], levels, preferred_element_type=jnp.float32).astype(jnp.bfloat16)
        cells = jnp.concatenate([cells[:modes], cells[modes:]], axis=1)
        for split in range(SPLITS):
            part = cells[split * share : (split + 1) * share]
            whole_ref, tail_ref, head_ref = outs[3 * split : 3 * split + 3]
            whole_ref[column] = part
            if column >= width - STEPS:
                tail_ref[column - width + STEPS] = part
            if column < STEPS:
                head_ref[column] = part


def project(blocks, basis, width):
    groups, rows, lanes = blocks.shape
    share = basis.shape[0] // 2 // SPLITS
    shapes = [jax.ShapeDtypeStruct((columns, share, 2 * lanes), jnp.bfloat16) for columns in (width, STEPS, STEPS)]
    return pl.pallas_call(
        functools.partial(project_kernel, width),
        out_shape=shapes * SPLITS,
        in_specs=[pl.BlockSpec(memory_space=pltpu.VMEM)] * 2,
        out_specs=[pl.BlockSpec(memory_space=pltpu.VMEM)] * (3 * SPLITS),
        scratch_shapes=[pltpu.VMEM((groups * rows + SPARE, lanes), jnp.float32)],
        compiler_params=pltpu.CompilerParams(vmem_limit_bytes=16 * 1024 * 1024),
        name="project",
    )(blocks, basis)


def expand_kernel(groups, basis_ref, *refs):
    parts, out_ref, held_ref = refs[:SPLITS], refs[SPLITS], refs[SPLITS + 1]
    width = parts[0].shape[0]
    rows, lanes = out_ref.shape[1:]
    for column in range(width):
        cells = [part[column, :, half * lanes : (half + 1) * lanes] for half in range(2) for part in parts]
        cells = jnp.concatenate(cells, axis=0)
        levels = jnp.dot(basis_ref[...], cells, preferred_element_type=jnp.float32)
        held_ref[pl.ds(column, groups * rows // width, stride=width), :] = levels
    for block in range(groups):
        out_ref[block] = held_ref[block * rows : (block + 1) * rows, :].astype(out_ref.dtype)


def expand(parts, basis, groups):
    width, share, lats = parts[0].shape
    rows = basis.shape[0] * width // groups
    return pl.pallas_call(
        functools.partial(expand_kernel, groups),
        out_shape=jax.ShapeDtypeStruct((groups, rows, lats // 2), jnp.bfloat16),
        in_specs=[pl.BlockSpec(memory_space=pltpu.VMEM)] * (SPLITS + 1),
        out_specs=pl.BlockSpec(memory_space=pltpu.VMEM),
        scratch_shapes=[pltpu.VMEM((groups * rows + SPARE, lats // 2), jnp.float32)],
        compiler_params=pltpu.CompilerParams(vmem_limit_bytes=16 * 1024 * 1024),
        name="expand",
    )(basis, *parts)


def paired(lats):
    row = lax.broadcasted_iota(jnp.int32, (lats, lats), 0)
    column = lax.broadcasted_iota(jnp.int32, (lats, lats), 1)
    half = lats // 2
    to = jnp.where(column < half, 2 * column, 2 * (column - half) + 1)
    back = jnp.where(row < half, 2 * row, 2 * (row - half) + 1)
    spread = jnp.where(row == to, 1.0, 0.0).astype(jnp.bfloat16)
    gather = jnp.where(column == back, 1.0, 0.0).astype(jnp.bfloat16)
    return spread, gather


def diffuse(modes_ref, left_ref, right_ref, kappa_ref, out_ref, u_ref, v_ref):
    width, count, lats = modes_ref.shape
    half = lats // 2
    total = width + 2 * STEPS
    spread, gather = paired(lats)

    def load(ref, at):
        cells = ref[...].reshape(ref.shape[0] * count, lats)
        cells = jnp.dot(cells, spread, preferred_element_type=jnp.float32)
        u_ref[at : at + ref.shape[0]] = cells.reshape(ref.shape[0], count, lats)

    load(left_ref, 0)
    load(modes_ref, STEPS)
    load(right_ref, STEPS + width)
    lane = lax.broadcasted_iota(jnp.int32, (count, half), 1)
    first, last = lane == 0, lane == half - 1
    kappa = kappa_ref[:, :half], kappa_ref[:, half:]
    keep = 1.0 - 4.0 * kappa[0], 1.0 - 4.0 * kappa[1]
    old, new = u_ref, v_ref
    for step in range(STEPS):
        before = old[step, :, :half], old[step, :, half:]
        here = old[step + 1, :, :half], old[step + 1, :, half:]
        for column in range(step + 1, total - step - 1):
            after = old[column + 1, :, :half], old[column + 1, :, half:]
            even, odd = here
            beside_even = odd + jnp.where(first, 0.0, pltpu.roll(odd, 1, 1))
            beside_odd = even + jnp.where(last, 0.0, pltpu.roll(even, half - 1, 1))
            new[column, :, :half] = keep[0] * even + kappa[0] * ((before[0] + after[0]) + beside_even)
            new[column, :, half:] = keep[1] * odd + kappa[1] * ((before[1] + after[1]) + beside_odd)
            before, here = here, after
        old, new = new, old
    cells = old[STEPS : STEPS + width].astype(jnp.bfloat16).reshape(width * count, lats)
    cells = jnp.dot(cells, gather, preferred_element_type=jnp.float32)
    out_ref[...] = cells.astype(out_ref.dtype).reshape(width, count, lats)


def diffused(modes, left, right, kappa):
    width, count, lats = modes.shape
    cells = pltpu.VMEM((width + 2 * STEPS, count, lats), jnp.float32)
    return pl.pallas_call(
        diffuse,
        out_shape=jax.ShapeDtypeStruct(modes.shape, jnp.bfloat16),
        in_specs=[pl.BlockSpec(memory_space=pltpu.VMEM)] * 4,
        out_specs=pl.BlockSpec(memory_space=pltpu.VMEM),
        scratch_shapes=[cells, cells],
        compiler_params=pltpu.CompilerParams(vmem_limit_bytes=16 * 1024 * 1024),
        cost_estimate=pl.CostEstimate(flops=60 * count * lats * (width + STEPS), bytes_accessed=6 * count * lats * width, transcendentals=0),
        name="diffuse",
    )(modes, left, right, kappa)


def on_device(field, eof_basis, band_of_mode, coef_table):
    groups, shards = lax.axis_size("lev"), lax.axis_size("lon")
    members, levels, lons, lats = field.shape
    pieces = groups // members
    width = lons // pieces
    count = eof_basis.shape[1]
    basis = basis_by_owner(THERE, eof_basis, groups, members)
    basis_back = basis_by_owner(BACK, eof_basis, groups, members)
    cut = pack(field, pieces)
    whole = exchange(THERE, cut, groups, shards, members)
    modes = project(whole, doubled(basis, groups).T, width)
    onward = loop_pairs(groups, shards, members)
    back = [(b, a) for a, b in onward]
    onehot = (band_of_mode[:, None] == jnp.arange(coef_table.shape[0])[None, :]).astype(jnp.float32)
    pairs = coef_table.reshape(-1, lats // 2, 2).transpose(0, 2, 1).reshape(coef_table.shape)
    kappa = jnp.dot(onehot, pairs, precision=lax.Precision.HIGHEST)
    share = count // SPLITS
    parts = []
    for split in range(SPLITS):
        some, tail, head = modes[3 * split : 3 * split + 3]
        left = lax.ppermute(tail, ("lev", "lon"), onward)
        right = lax.ppermute(head, ("lev", "lon"), back)
        parts.append(diffused(some, left, right, kappa[split * share : (split + 1) * share]))
    total = expand(parts, doubled(basis_back, groups), groups)
    total = exchange(BACK, total, groups, shards, members)
    return unpack(total, field.shape, pieces)


def solution(mesh):
    return jax.shard_map(
        on_device,
        mesh=mesh,
        in_specs=(P(None, "lev", "lon", None), P(), P(), P()),
        out_specs=P(None, "lev", "lon", None),
        check_vma=False,
    )
```

```python
import functools

import jax
import jax.numpy as jnp
from jax import lax
from jax.experimental import pallas as pl
from jax.experimental.pallas import tpu as pltpu
from jax.sharding import PartitionSpec as P

STEPS = 8
LANES = 128
SPARE = 16
THERE = (15, 10, 8, 2, 12, 6, 5, 0, 14, 4, 9, 11, 13, 7, 3, 1)
BACK = (15, 10, 8, 2, 12, 6, 5, 0, 14, 4, 7, 3, 13, 9, 11, 1)
SPLITS = 2


def place(piece, shard, pieces):
    return piece + ((shard + 1) % 2) * (pieces - 1 - 2 * piece)


def loop_pairs(groups, shards, members):
    pieces = groups // members
    pairs = []
    for shard in range(shards):
        for piece in range(pieces):
            for member in range(members):
                carry, after = divmod(piece + 1, pieces)
                then = (shard + carry) % shards
                here = place(piece, shard, pieces) * members + member
                there = place(after, then, pieces) * members + member
                pairs.append((here * shards + shard, there * shards + then))
    return pairs


def slot(order, member, piece, members):
    return order.index(piece * members + member)


def owners(order, shard, pieces, members):
    return [place(cell // members, shard, pieces) * members + cell % members for cell in order]


def exchange(order, blocks, groups, shards, members):
    devices = [[lev * shards + shard for lev in owners(order, shard, groups // members, members)] for shard in range(shards)]
    return lax.all_to_all(blocks, ("lev", "lon"), 0, 0, tiled=True, axis_index_groups=devices)


def basis_by_owner(order, basis, groups, members):
    rows = basis.shape[0] // groups

    def ordered(shard):
        found = owners(order, shard, groups // members, members)
        return jnp.concatenate([basis[lev * rows : (lev + 1) * rows] for lev in found])

    return jnp.where(lax.axis_index("lon") % 2 == 0, ordered(0), ordered(1))


def pack_kernel(pieces, field_ref, out_ref, held_ref, sems):
    members, levels, lons, lats = field_ref.shape
    width = lons // pieces
    copies = []
    for member in range(members):
        for piece in range(pieces):
            to = slot(THERE, member, piece, members)
            for level in range(levels):
                for half in range(lats // LANES):
                    row = (half * levels + level) * width
                    columns = slice(half * LANES, (half + 1) * LANES)
                    held_ref[to, row : row + width, :] = field_ref[member, level, piece * width : (piece + 1) * width, columns]
            copy = pltpu.make_async_copy(held_ref.at[to], out_ref.at[to], sems.at[to])
            copy.start()
            copies.append(copy)
    for copy in copies:
        copy.wait()


def pack(field, pieces):
    members, levels, lons, lats = field.shape
    shape = (pieces * members, levels * (lons // pieces) * lats // LANES, LANES)
    return pl.pallas_call(
        functools.partial(pack_kernel, pieces),
        out_shape=jax.ShapeDtypeStruct(shape, field.dtype),
        in_specs=[pl.BlockSpec(memory_space=pltpu.VMEM)],
        out_specs=pl.BlockSpec(memory_space=pl.ANY),
        scratch_shapes=[pltpu.VMEM(shape, field.dtype), pltpu.SemaphoreType.DMA((pieces * members,))],
        compiler_params=pltpu.CompilerParams(vmem_limit_bytes=16 * 1024 * 1024),
        name="pack",
    )(field)


def unpack_kernel(pieces, blocks_ref, out_ref, held_ref, sems):
    members, levels, lons, lats = out_ref.shape
    width = lons // pieces
    copies = []
    for level in range(levels):
        for member in range(members):
            for piece in range(pieces):
                at = slot(BACK, member, piece, members)
                for half in range(lats // LANES):
                    row = (half * levels + level) * width
                    columns = slice(half * LANES, (half + 1) * LANES)
                    held_ref[member, level, piece * width : (piece + 1) * width, columns] = blocks_ref[at, row : row + width, :]
            copy = pltpu.make_async_copy(held_ref.at[member, level], out_ref.at[member, level], sems.at[member, level])
            copy.start()
            copies.append(copy)
    for copy in copies:
        copy.wait()


def unpack(blocks, shape, pieces):
    members, levels, lons, lats = shape
    return pl.pallas_call(
        functools.partial(unpack_kernel, pieces),
        out_shape=jax.ShapeDtypeStruct(shape, blocks.dtype),
        in_specs=[pl.BlockSpec(memory_space=pltpu.VMEM)],
        out_specs=pl.BlockSpec(memory_space=pl.ANY),
        scratch_shapes=[pltpu.VMEM(shape, blocks.dtype), pltpu.SemaphoreType.DMA((members, levels))],
        compiler_params=pltpu.CompilerParams(vmem_limit_bytes=16 * 1024 * 1024),
        name="unpack",
    )(blocks)


def doubled(basis, groups):
    rows = basis.reshape(groups, 1, -1, 1, basis.shape[1])
    same = jnp.eye(2, dtype=basis.dtype).reshape(1, 2, 1, 2, 1)
    return (rows * same).reshape(2 * basis.shape[0], 2 * basis.shape[1])


def project_kernel(width, blocks_ref, basis_ref, *refs):
    outs, held_ref = refs[:-1], refs[-1]
    groups, rows, lanes = blocks_ref.shape
    modes = basis_ref.shape[0] // 2
    share = modes // SPLITS
    for block in range(groups):
        held_ref[block * rows : (block + 1) * rows, :] = blocks_ref[block].astype(jnp.float32)
    for column in range(width):
        levels = held_ref[pl.ds(column, groups * rows // width, stride=width), :].astype(jnp.bfloat16)
        cells = jnp.dot(basis_ref[...], levels, preferred_element_type=jnp.float32).astype(jnp.bfloat16)
        cells = jnp.concatenate([cells[:modes], cells[modes:]], axis=1)
        for split in range(SPLITS):
            part = cells[split * share : (split + 1) * share]
            whole_ref, tail_ref, head_ref = outs[3 * split : 3 * split + 3]
            whole_ref[column] = part
            if column >= width - STEPS:
                tail_ref[column - width + STEPS] = part
            if column < STEPS:
                head_ref[column] = part


def project(blocks, basis, width):
    groups, rows, lanes = blocks.shape
    share = basis.shape[0] // 2 // SPLITS
    shapes = [jax.ShapeDtypeStruct((columns, share, 2 * lanes), jnp.bfloat16) for columns in (width, STEPS, STEPS)]
    return pl.pallas_call(
        functools.partial(project_kernel, width),
        out_shape=shapes * SPLITS,
        in_specs=[pl.BlockSpec(memory_space=pltpu.VMEM)] * 2,
        out_specs=[pl.BlockSpec(memory_space=pltpu.VMEM)] * (3 * SPLITS),
        scratch_shapes=[pltpu.VMEM((groups * rows + SPARE, lanes), jnp.float32)],
        compiler_params=pltpu.CompilerParams(vmem_limit_bytes=16 * 1024 * 1024),
        name="project",
    )(blocks, basis)


def expand_kernel(groups, basis_ref, *refs):
    parts, out_ref, held_ref = refs[:SPLITS], refs[SPLITS], refs[SPLITS + 1]
    width = parts[0].shape[0]
    rows, lanes = out_ref.shape[1:]
    for column in range(width):
        cells = [part[column, :, half * lanes : (half + 1) * lanes] for half in range(2) for part in parts]
        cells = jnp.concatenate(cells, axis=0)
        levels = jnp.dot(basis_ref[...], cells, preferred_element_type=jnp.float32)
        held_ref[pl.ds(column, groups * rows // width, stride=width), :] = levels
    for block in range(groups):
        out_ref[block] = held_ref[block * rows : (block + 1) * rows, :].astype(out_ref.dtype)


def expand(parts, basis, groups):
    width, share, lats = parts[0].shape
    rows = basis.shape[0] * width // groups
    return pl.pallas_call(
        functools.partial(expand_kernel, groups),
        out_shape=jax.ShapeDtypeStruct((groups, rows, lats // 2), jnp.bfloat16),
        in_specs=[pl.BlockSpec(memory_space=pltpu.VMEM)] * (SPLITS + 1),
        out_specs=pl.BlockSpec(memory_space=pltpu.VMEM),
        scratch_shapes=[pltpu.VMEM((groups * rows + SPARE, lats // 2), jnp.float32)],
        compiler_params=pltpu.CompilerParams(vmem_limit_bytes=16 * 1024 * 1024),
        name="expand",
    )(basis, *parts)


def paired(lats):
    row = lax.broadcasted_iota(jnp.int32, (lats, lats), 0)
    column = lax.broadcasted_iota(jnp.int32, (lats, lats), 1)
    half = lats // 2
    to = jnp.where(column < half, 2 * column, 2 * (column - half) + 1)
    back = jnp.where(row < half, 2 * row, 2 * (row - half) + 1)
    spread = jnp.where(row == to, 1.0, 0.0).astype(jnp.bfloat16)
    gather = jnp.where(column == back, 1.0, 0.0).astype(jnp.bfloat16)
    return spread, gather


def update(get, put, kappa, keep, level, columns, half):
    lane = lax.broadcasted_iota(jnp.int32, kappa[0].shape, 1)
    first, last = lane == 0, lane == half - 1
    for column in columns:
        before, (even, odd), after = get(level, column - 1), get(level, column), get(level, column + 1)
        beside_even = odd + jnp.where(first, 0.0, pltpu.roll(odd, 1, 1))
        beside_odd = even + jnp.where(last, 0.0, pltpu.roll(even, half - 1, 1))
        put(level + 1, column, 0, keep[0] * even + kappa[0] * ((before[0] + after[0]) + beside_even))
        put(level + 1, column, 1, keep[1] * odd + kappa[1] * ((before[1] + after[1]) + beside_odd))


def coefficients(kappa_ref, half):
    kappa = kappa_ref[:, :half], kappa_ref[:, half:]
    return kappa, (1.0 - 4.0 * kappa[0], 1.0 - 4.0 * kappa[1])


def inner_kernel(modes_ref, kappa_ref, inner_ref):
    width, count, lats = modes_ref.shape
    half = lats // 2
    spread, _ = paired(lats)
    cells = jnp.dot(modes_ref[...].reshape(width * count, lats), spread, preferred_element_type=jnp.float32)
    inner_ref[0] = cells.reshape(width, count, lats)
    kappa, keep = coefficients(kappa_ref, half)

    def get(level, column):
        return inner_ref[level, column, :, :half], inner_ref[level, column, :, half:]

    def put(level, column, side, value):
        inner_ref[level, column, :, side * half : (side + 1) * half] = value

    for level in range(inner_ref.shape[0] - 1):
        update(get, put, kappa, keep, level, range(level + 1, width - level - 1), half)


def outer_kernel(inner_ref, left_ref, right_ref, kappa_ref, out_ref, u_ref, v_ref):
    levels, width, count, lats = inner_ref.shape
    half = lats // 2
    total = width + 2 * STEPS
    spread, gather = paired(lats)
    for ref, at in ((left_ref, 0), (right_ref, STEPS + width)):
        cells = jnp.dot(ref[...].reshape(STEPS * count, lats), spread, preferred_element_type=jnp.float32)
        u_ref[at : at + STEPS] = cells.reshape(STEPS, count, lats)
    kappa, keep = coefficients(kappa_ref, half)

    def known(level, column):
        return level < levels and STEPS + level <= column < STEPS + width - level

    def get(level, column):
        if known(level, column):
            return inner_ref[level, column - STEPS, :, :half], inner_ref[level, column - STEPS, :, half:]
        ref = v_ref if level % 2 else u_ref
        return ref[column, :, :half], ref[column, :, half:]

    def put(level, column, side, value):
        ref = v_ref if level % 2 else u_ref
        ref[column, :, side * half : (side + 1) * half] = value

    for level in range(STEPS):
        columns = [c for c in range(level + 1, total - level - 1) if not known(level + 1, c)]
        update(get, put, kappa, keep, level, columns, half)
    final = v_ref if STEPS % 2 else u_ref
    cells = final[STEPS : STEPS + width].astype(jnp.bfloat16).reshape(width * count, lats)
    cells = jnp.dot(cells, gather, preferred_element_type=jnp.float32)
    out_ref[...] = cells.astype(out_ref.dtype).reshape(width, count, lats)


def inner(modes, kappa):
    width, count, lats = modes.shape
    levels = min((width - 1) // 2, STEPS - 1) + 1
    return pl.pallas_call(
        inner_kernel,
        out_shape=jax.ShapeDtypeStruct((levels, width, count, lats), jnp.float32),
        in_specs=[pl.BlockSpec(memory_space=pltpu.VMEM)] * 2,
        out_specs=pl.BlockSpec(memory_space=pltpu.VMEM),
        compiler_params=pltpu.CompilerParams(vmem_limit_bytes=16 * 1024 * 1024),
        cost_estimate=pl.CostEstimate(flops=16 * count * lats * width, bytes_accessed=6 * count * lats * width, transcendentals=0),
        name="inner",
    )(modes, kappa)


def diffused(known, left, right, kappa):
    levels, width, count, lats = known.shape
    cells = pltpu.VMEM((width + 2 * STEPS, count, lats), jnp.float32)
    return pl.pallas_call(
        outer_kernel,
        out_shape=jax.ShapeDtypeStruct((width, count, lats), jnp.bfloat16),
        in_specs=[pl.BlockSpec(memory_space=pltpu.VMEM)] * 4,
        out_specs=pl.BlockSpec(memory_space=pltpu.VMEM),
        scratch_shapes=[cells, cells],
        compiler_params=pltpu.CompilerParams(vmem_limit_bytes=16 * 1024 * 1024),
        cost_estimate=pl.CostEstimate(flops=60 * count * lats * (width + STEPS), bytes_accessed=6 * count * lats * width, transcendentals=0),
        name="diffuse",
    )(known, left, right, kappa)


def on_device(field, eof_basis, band_of_mode, coef_table):
    groups, shards = lax.axis_size("lev"), lax.axis_size("lon")
    members, levels, lons, lats = field.shape
    pieces = groups // members
    width = lons // pieces
    count = eof_basis.shape[1]
    basis = basis_by_owner(THERE, eof_basis, groups, members)
    basis_back = basis_by_owner(BACK, eof_basis, groups, members)
    cut = pack(field, pieces)
    whole = exchange(THERE, cut, groups, shards, members)
    modes = project(whole, doubled(basis, groups).T, width)
    onward = loop_pairs(groups, shards, members)
    back = [(b, a) for a, b in onward]
    onehot = (band_of_mode[:, None] == jnp.arange(coef_table.shape[0])[None, :]).astype(jnp.float32)
    pairs = coef_table.reshape(-1, lats // 2, 2).transpose(0, 2, 1).reshape(coef_table.shape)
    kappa = jnp.dot(onehot, pairs, precision=lax.Precision.HIGHEST)
    share = count // SPLITS
    parts = []
    for split in range(SPLITS):
        some, tail, head = modes[3 * split : 3 * split + 3]
        left = lax.ppermute(tail, ("lev", "lon"), onward)
        right = lax.ppermute(head, ("lev", "lon"), back)
        some_kappa = kappa[split * share : (split + 1) * share]
        parts.append(diffused(inner(some, some_kappa), left, right, some_kappa))
    total = expand(parts, doubled(basis_back, groups), groups)
    total = exchange(BACK, total, groups, shards, members)
    return unpack(total, field.shape, pieces)


def solution(mesh):
    return jax.shard_map(
        on_device,
        mesh=mesh,
        in_specs=(P(None, "lev", "lon", None), P(), P(), P()),
        out_specs=P(None, "lev", "lon", None),
        check_vma=False,
    )
```

```python
import functools

import jax
import jax.numpy as jnp
from jax import lax
from jax.experimental import pallas as pl
from jax.experimental.pallas import tpu as pltpu
from jax.sharding import PartitionSpec as P

STEPS = 8
LANES = 128
SPARE = 16
THERE = (15, 10, 8, 2, 12, 6, 5, 0, 14, 4, 7, 3, 13, 9, 11, 1)
BACK = (15, 10, 8, 2, 12, 6, 5, 0, 14, 4, 7, 3, 13, 9, 11, 1)
SPLITS = 2


def place(piece, shard, pieces):
    return piece + ((shard + 1) % 2) * (pieces - 1 - 2 * piece)


def loop_pairs(groups, shards, members):
    pieces = groups // members
    pairs = []
    for shard in range(shards):
        for piece in range(pieces):
            for member in range(members):
                carry, after = divmod(piece + 1, pieces)
                then = (shard + carry) % shards
                here = place(piece, shard, pieces) * members + member
                there = place(after, then, pieces) * members + member
                pairs.append((here * shards + shard, there * shards + then))
    return pairs


def slot(order, member, piece, members):
    return order.index(piece * members + member)


def owners(order, shard, pieces, members):
    return [place(cell // members, shard, pieces) * members + cell % members for cell in order]


def exchange(order, blocks, groups, shards, members):
    devices = [[lev * shards + shard for lev in owners(order, shard, groups // members, members)] for shard in range(shards)]
    return lax.all_to_all(blocks, ("lev", "lon"), 0, 0, tiled=True, axis_index_groups=devices)


def basis_by_owner(order, basis, groups, members):
    rows = basis.shape[0] // groups

    def ordered(shard):
        found = owners(order, shard, groups // members, members)
        return jnp.concatenate([basis[lev * rows : (lev + 1) * rows] for lev in found])

    return jnp.where(lax.axis_index("lon") % 2 == 0, ordered(0), ordered(1))


def pack_kernel(pieces, field_ref, out_ref, held_ref, sems):
    members, levels, lons, lats = field_ref.shape
    width = lons // pieces
    copies = []
    for member in range(members):
        for piece in range(pieces):
            to = slot(THERE, member, piece, members)
            for level in range(levels):
                for half in range(lats // LANES):
                    row = (half * levels + level) * width
                    columns = slice(half * LANES, (half + 1) * LANES)
                    held_ref[to, row : row + width, :] = field_ref[member, level, piece * width : (piece + 1) * width, columns]
            copy = pltpu.make_async_copy(held_ref.at[to], out_ref.at[to], sems.at[to])
            copy.start()
            copies.append(copy)
    for copy in copies:
        copy.wait()


def pack(field, pieces):
    members, levels, lons, lats = field.shape
    shape = (pieces * members, levels * (lons // pieces) * lats // LANES, LANES)
    return pl.pallas_call(
        functools.partial(pack_kernel, pieces),
        out_shape=jax.ShapeDtypeStruct(shape, field.dtype),
        in_specs=[pl.BlockSpec(memory_space=pltpu.VMEM)],
        out_specs=pl.BlockSpec(memory_space=pl.ANY),
        scratch_shapes=[pltpu.VMEM(shape, field.dtype), pltpu.SemaphoreType.DMA((pieces * members,))],
        compiler_params=pltpu.CompilerParams(vmem_limit_bytes=16 * 1024 * 1024),
        name="pack",
    )(field)


def unpack_kernel(pieces, blocks_ref, out_ref, held_ref, sems):
    members, levels, lons, lats = out_ref.shape
    width = lons // pieces
    copies = []
    for level in range(levels):
        for member in range(members):
            for piece in range(pieces):
                at = slot(BACK, member, piece, members)
                for half in range(lats // LANES):
                    row = (half * levels + level) * width
                    columns = slice(half * LANES, (half + 1) * LANES)
                    held_ref[member, level, piece * width : (piece + 1) * width, columns] = blocks_ref[at, row : row + width, :]
            copy = pltpu.make_async_copy(held_ref.at[member, level], out_ref.at[member, level], sems.at[member, level])
            copy.start()
            copies.append(copy)
    for copy in copies:
        copy.wait()


def unpack(blocks, shape, pieces):
    members, levels, lons, lats = shape
    return pl.pallas_call(
        functools.partial(unpack_kernel, pieces),
        out_shape=jax.ShapeDtypeStruct(shape, blocks.dtype),
        in_specs=[pl.BlockSpec(memory_space=pltpu.VMEM)],
        out_specs=pl.BlockSpec(memory_space=pl.ANY),
        scratch_shapes=[pltpu.VMEM(shape, blocks.dtype), pltpu.SemaphoreType.DMA((members, levels))],
        compiler_params=pltpu.CompilerParams(vmem_limit_bytes=16 * 1024 * 1024),
        name="unpack",
    )(blocks)


def doubled(basis, groups):
    rows = basis.reshape(groups, 1, -1, 1, basis.shape[1])
    same = jnp.eye(2, dtype=basis.dtype).reshape(1, 2, 1, 2, 1)
    return (rows * same).reshape(2 * basis.shape[0], 2 * basis.shape[1])


def project_kernel(width, blocks_ref, basis_ref, *refs):
    outs, held_ref = refs[:-1], refs[-1]
    groups, rows, lanes = blocks_ref.shape
    modes = basis_ref.shape[0] // 2
    share = modes // SPLITS
    for block in range(groups):
        held_ref[block * rows : (block + 1) * rows, :] = blocks_ref[block].astype(jnp.float32)
    for column in range(width):
        levels = held_ref[pl.ds(column, groups * rows // width, stride=width), :].astype(jnp.bfloat16)
        cells = jnp.dot(basis_ref[...], levels, preferred_element_type=jnp.float32).astype(jnp.bfloat16)
        cells = jnp.concatenate([cells[:modes], cells[modes:]], axis=1)
        for split in range(SPLITS):
            part = cells[split * share : (split + 1) * share]
            whole_ref, tail_ref, head_ref = outs[3 * split : 3 * split + 3]
            whole_ref[column] = part
            if column >= width - STEPS:
                tail_ref[column - width + STEPS] = part
            if column < STEPS:
                head_ref[column] = part


def project(blocks, basis, width):
    groups, rows, lanes = blocks.shape
    share = basis.shape[0] // 2 // SPLITS
    shapes = [jax.ShapeDtypeStruct((columns, share, 2 * lanes), jnp.bfloat16) for columns in (width, STEPS, STEPS)]
    return pl.pallas_call(
        functools.partial(project_kernel, width),
        out_shape=shapes * SPLITS,
        in_specs=[pl.BlockSpec(memory_space=pltpu.VMEM)] * 2,
        out_specs=[pl.BlockSpec(memory_space=pltpu.VMEM)] * (3 * SPLITS),
        scratch_shapes=[pltpu.VMEM((groups * rows + SPARE, lanes), jnp.float32)],
        compiler_params=pltpu.CompilerParams(vmem_limit_bytes=16 * 1024 * 1024),
        name="project",
    )(blocks, basis)


def expand_kernel(groups, basis_ref, *refs):
    parts, out_ref, held_ref = refs[:SPLITS], refs[SPLITS], refs[SPLITS + 1]
    width = parts[0].shape[0]
    rows, lanes = out_ref.shape[1:]
    for column in range(width):
        cells = [part[column, :, half * lanes : (half + 1) * lanes] for half in range(2) for part in parts]
        cells = jnp.concatenate(cells, axis=0)
        levels = jnp.dot(basis_ref[...], cells, preferred_element_type=jnp.float32)
        held_ref[pl.ds(column, groups * rows // width, stride=width), :] = levels
    for block in range(groups):
        out_ref[block] = held_ref[block * rows : (block + 1) * rows, :].astype(out_ref.dtype)


def expand(parts, basis, groups):
    width, share, lats = parts[0].shape
    rows = basis.shape[0] * width // groups
    return pl.pallas_call(
        functools.partial(expand_kernel, groups),
        out_shape=jax.ShapeDtypeStruct((groups, rows, lats // 2), jnp.bfloat16),
        in_specs=[pl.BlockSpec(memory_space=pltpu.VMEM)] * (SPLITS + 1),
        out_specs=pl.BlockSpec(memory_space=pltpu.VMEM),
        scratch_shapes=[pltpu.VMEM((groups * rows + SPARE, lats // 2), jnp.float32)],
        compiler_params=pltpu.CompilerParams(vmem_limit_bytes=16 * 1024 * 1024),
        name="expand",
    )(basis, *parts)


def paired(lats):
    row = lax.broadcasted_iota(jnp.int32, (lats, lats), 0)
    column = lax.broadcasted_iota(jnp.int32, (lats, lats), 1)
    half = lats // 2
    to = jnp.where(column < half, 2 * column, 2 * (column - half) + 1)
    back = jnp.where(row < half, 2 * row, 2 * (row - half) + 1)
    spread = jnp.where(row == to, 1.0, 0.0).astype(jnp.bfloat16)
    gather = jnp.where(column == back, 1.0, 0.0).astype(jnp.bfloat16)
    return spread, gather


def update(get, put, kappa, keep, level, columns, half):
    lane = lax.broadcasted_iota(jnp.int32, kappa[0].shape, 1)
    first, last = lane == 0, lane == half - 1
    for column in columns:
        before, (even, odd), after = get(level, column - 1), get(level, column), get(level, column + 1)
        beside_even = odd + jnp.where(first, 0.0, pltpu.roll(odd, 1, 1))
        beside_odd = even + jnp.where(last, 0.0, pltpu.roll(even, half - 1, 1))
        put(level + 1, column, 0, keep[0] * even + kappa[0] * ((before[0] + after[0]) + beside_even))
        put(level + 1, column, 1, keep[1] * odd + kappa[1] * ((before[1] + after[1]) + beside_odd))


def coefficients(kappa_ref, half):
    kappa = kappa_ref[:, :half], kappa_ref[:, half:]
    return kappa, (1.0 - 4.0 * kappa[0], 1.0 - 4.0 * kappa[1])


def inner_kernel(modes_ref, kappa_ref, inner_ref):
    width, count, lats = modes_ref.shape
    half = lats // 2
    spread, _ = paired(lats)
    cells = jnp.dot(modes_ref[...].reshape(width * count, lats), spread, preferred_element_type=jnp.float32)
    inner_ref[0] = cells.reshape(width, count, lats)
    kappa, keep = coefficients(kappa_ref, half)

    def get(level, column):
        return inner_ref[level, column, :, :half], inner_ref[level, column, :, half:]

    def put(level, column, side, value):
        inner_ref[level, column, :, side * half : (side + 1) * half] = value

    for level in range(inner_ref.shape[0] - 1):
        update(get, put, kappa, keep, level, range(level + 1, width - level - 1), half)


def outer_kernel(inner_ref, left_ref, right_ref, kappa_ref, out_ref, u_ref, v_ref):
    levels, width, count, lats = inner_ref.shape
    half = lats // 2
    total = width + 2 * STEPS
    spread, gather = paired(lats)
    for ref, at in ((left_ref, 0), (right_ref, STEPS + width)):
        cells = jnp.dot(ref[...].reshape(STEPS * count, lats), spread, preferred_element_type=jnp.float32)
        u_ref[at : at + STEPS] = cells.reshape(STEPS, count, lats)
    kappa, keep = coefficients(kappa_ref, half)

    def known(level, column):
        return level < levels and STEPS + level <= column < STEPS + width - level

    def get(level, column):
        if known(level, column):
            return inner_ref[level, column - STEPS, :, :half], inner_ref[level, column - STEPS, :, half:]
        ref = v_ref if level % 2 else u_ref
        return ref[column, :, :half], ref[column, :, half:]

    def put(level, column, side, value):
        ref = v_ref if level % 2 else u_ref
        ref[column, :, side * half : (side + 1) * half] = value

    for level in range(STEPS):
        columns = [c for c in range(level + 1, total - level - 1) if not known(level + 1, c)]
        update(get, put, kappa, keep, level, columns, half)
    final = v_ref if STEPS % 2 else u_ref
    cells = final[STEPS : STEPS + width].astype(jnp.bfloat16).reshape(width * count, lats)
    cells = jnp.dot(cells, gather, preferred_element_type=jnp.float32)
    out_ref[...] = cells.astype(out_ref.dtype).reshape(width, count, lats)


def inner(modes, kappa):
    width, count, lats = modes.shape
    levels = min((width - 1) // 2, STEPS - 1) + 1
    return pl.pallas_call(
        inner_kernel,
        out_shape=jax.ShapeDtypeStruct((levels, width, count, lats), jnp.float32),
        in_specs=[pl.BlockSpec(memory_space=pltpu.VMEM)] * 2,
        out_specs=pl.BlockSpec(memory_space=pltpu.VMEM),
        compiler_params=pltpu.CompilerParams(vmem_limit_bytes=16 * 1024 * 1024),
        cost_estimate=pl.CostEstimate(flops=16 * count * lats * width, bytes_accessed=6 * count * lats * width, transcendentals=0),
        name="inner",
    )(modes, kappa)


def diffused(known, left, right, kappa):
    levels, width, count, lats = known.shape
    cells = pltpu.VMEM((width + 2 * STEPS, count, lats), jnp.float32)
    return pl.pallas_call(
        outer_kernel,
        out_shape=jax.ShapeDtypeStruct((width, count, lats), jnp.bfloat16),
        in_specs=[pl.BlockSpec(memory_space=pltpu.VMEM)] * 4,
        out_specs=pl.BlockSpec(memory_space=pltpu.VMEM),
        scratch_shapes=[cells, cells],
        compiler_params=pltpu.CompilerParams(vmem_limit_bytes=16 * 1024 * 1024),
        cost_estimate=pl.CostEstimate(flops=60 * count * lats * (width + STEPS), bytes_accessed=6 * count * lats * width, transcendentals=0),
        name="diffuse",
    )(known, left, right, kappa)


def on_device(field, eof_basis, band_of_mode, coef_table):
    groups, shards = lax.axis_size("lev"), lax.axis_size("lon")
    members, levels, lons, lats = field.shape
    pieces = groups // members
    width = lons // pieces
    count = eof_basis.shape[1]
    basis = basis_by_owner(THERE, eof_basis, groups, members)
    basis_back = basis_by_owner(BACK, eof_basis, groups, members)
    cut = pack(field, pieces)
    whole = exchange(THERE, cut, groups, shards, members)
    modes = project(whole, doubled(basis, groups).T, width)
    onward = loop_pairs(groups, shards, members)
    back = [(b, a) for a, b in onward]
    onehot = (band_of_mode[:, None] == jnp.arange(coef_table.shape[0])[None, :]).astype(jnp.float32)
    pairs = coef_table.reshape(-1, lats // 2, 2).transpose(0, 2, 1).reshape(coef_table.shape)
    kappa = jnp.dot(onehot, pairs, precision=lax.Precision.HIGHEST)
    share = count // SPLITS
    parts = []
    for split in range(SPLITS):
        some, tail, head = modes[3 * split : 3 * split + 3]
        left = lax.ppermute(tail, ("lev", "lon"), onward)
        right = lax.ppermute(head, ("lev", "lon"), back)
        some_kappa = kappa[split * share : (split + 1) * share]
        parts.append(diffused(inner(some, some_kappa), left, right, some_kappa))
    total = expand(parts, doubled(basis_back, groups), groups)
    total = exchange(BACK, total, groups, shards, members)
    return unpack(total, field.shape, pieces)


def solution(mesh):
    return jax.shard_map(
        on_device,
        mesh=mesh,
        in_specs=(P(None, "lev", "lon", None), P(), P(), P()),
        out_specs=P(None, "lev", "lon", None),
        check_vma=False,
    )
```
